256 devices in a mesh: dp: 32 (over x, z_hi, core), head: 8 (over z_lo, y).
Axes of the slice: x: 4, y: 4, z: 8 (z_hi: 4, z_lo: 2; z = z_hi * 2 + z_lo), core: 2. Of those that a mesh axis runs over, the one named last changes fastest.
Arguments:
- q_nope: bfloat16 [256, 4, 16384], P('dp', None, 'head'), may hold values from -120 to 120
- q_rope: bfloat16 [256, 4, 8192], P('dp', None, 'head'), may hold values from -6 to 6
- new_latent: bfloat16 [256, 4, 512], P('dp'), may hold values from -6 to 6
- new_rope: bfloat16 [256, 4, 64], P('dp'), may hold values from -6 to 6
- pool_latent: bfloat16 [2048, 64, 512], P('dp', 'head'), may hold values from -6 to 6
- pool_rope: bfloat16 [2048, 4096], P('dp', 'head'), may hold values from -6 to 6
- kv_weight: bfloat16 [512, 128, 256], P('dp', 'head'), may hold values from -0.25 to 0.25
- src_dev: int32 [4096, 1], P('dp'), may hold values from 0 to 31; in each aligned block of 128 rows (0 to 127, 128 to 255, ...) at most 5 rows name the same one
- src_block: int32 [4096], P('dp'), may hold values from 0 to 63
- lengths: int32 [256], P('dp'), may hold values from 1 to 1024
Outputs:
- attn_out: bfloat16 [256, 4, 16384], P('dp', None, 'head')
The draws below stay inside these ranges and needn't reach their ends.
Inputs may be any that keep to these rules, and one draw needn't show every extreme that they name: `src_dev`: among the 128 table entries of one index of dp, at most 5 name the same index of dp, a bound that some block reaches.
All inputs are finite; a program needn't handle non-finite values.
Results may differ from the reference program's by a relative error of at most 0.006.
The reference program's roundings to bfloat16 on the way count: a program that leaves them out, or rounds other values in their place, can miss the bound.
Values may be sent and summed in bfloat16 or wider, within the bound.
A program may use at most 128 MiB of HBM per device.

```python
import math
import jax
import jax.numpy as jnp
import numpy as np
from jax import lax

LAT = 512
ROPE = 64
NOPE = 128
DV = 128
STEPS = 4
BLK = 64
MAXB = 16
REQ_DEV = 8
POOL_DEV = 64
CAP = 5
HEADS = 128
REQS = 256
POOLS = 2048
N_DP = 32


def draw_q_nope(key, part):
    key = jax.random.fold_in(key, 11)
    shape = (REQS, STEPS, HEADS, NOPE)
    values = jnp.clip(jax.random.normal(key, shape, jnp.float32), -6.0, 6.0)
    return values.reshape(REQS, STEPS, HEADS * NOPE).astype(jnp.bfloat16)


def draw_lengths(key, part):
    key = jax.random.fold_in(key, 5)
    drawn = jax.random.randint(key, (REQS,), 1, MAXB * BLK + 1)
    return drawn.at[0].set(MAXB * BLK).astype(jnp.int32)


def place_ends(array, stream_key, low, high):
    index_at = [jax.random.randint(jax.random.fold_in(stream_key, axis), (), 0, length) for axis, length in enumerate(array.shape)]
    main_axis = array.shape.index(max(array.shape))
    beside = index_at[:main_axis] + [(index_at[main_axis] + 1) % array.shape[main_axis]] + index_at[main_axis + 1:]
    return array.at[tuple(index_at)].set(low).at[tuple(beside)].set(high)


def steps_of(key, dims, shards, smallest, top_value):
    def one(dim, blocks):
        steps = jax.random.uniform(jax.random.fold_in(jax.random.fold_in(key, 6), dim), (blocks,), jnp.float32, smallest / len(shards), top_value / len(shards))
        return jnp.repeat(jnp.exp(steps), dims[dim] // blocks).reshape((-1,) + (1,) * (len(dims) - dim - 1))

    loudness = one(*shards[0])
    for cut in shards[1:]:
        loudness = loudness * one(*cut)
    return loudness


def shared_out(own_key, own, number, rows, amount, top, bound, skew):
    order = jax.random.permutation(own_key, amount)
    packed, usual = shares(amount, rows * top, bound, skew, True), shares(amount, rows * top, bound, skew, False)
    places = jnp.arange(amount)

    def named(tallies, offset_by):
        used = int((tallies > 0).sum())
        fixed = max(1, used // 4)
        passed = fixed + (places - fixed + offset_by * (used - fixed)) % max(1, amount - fixed)
        return jnp.zeros((amount,), jnp.int32).at[order[jnp.where(places < fixed, places, passed)]].set(jnp.asarray(tallies, jnp.int32))

    tallies = jnp.where(number % 4 == 0, named(packed, number // 4), named(usual, number - number // 4 - 1))
    mixed = jax.random.permutation(jax.random.fold_in(own, 3), amount)
    source_of, taker = mixed[0:amount // 2 * 2:2], mixed[1:amount // 2 * 2:2]
    room = jnp.minimum(tallies[source_of] - 1, bound - tallies[taker]) // 2
    room = jnp.where((source_of == order[0]) | (taker == order[0]) | (tallies[taker] == 0), 0, jnp.maximum(room, 0))
    passed = jax.random.randint(jax.random.fold_in(own, 4), (amount // 2,), 0, 1 << 20) % (room + 1)
    tallies = tallies.at[source_of].add(-passed).at[taker].add(passed)
    labels = jnp.searchsorted(jnp.cumsum(tallies), jnp.arange(rows * top), side="right").astype(jnp.int32)
    listing = labels.reshape(top, rows).T
    listing = listing[jax.random.permutation(jax.random.fold_in(own, 1), rows)]
    offset_by = jax.random.randint(jax.random.fold_in(own, 2), (rows, 1), 0, top)
    return jnp.take_along_axis(listing, (jnp.arange(top)[None, :] + offset_by) % top, axis=1)


def shares(number_of, total, bound, slope, full):
    loads = [(1 << 20) // math.isqrt(grade ** slope) + 1 for grade in range(1, number_of + 1)]
    largest = bound if full else min(bound, max(-(-total // number_of), total * loads[0] // sum(loads)))
    least = 1 if total - largest >= number_of - 1 else 0
    counts, surplus = [largest] + [least] * (number_of - 1), total - largest - least * (number_of - 1)
    while surplus > 0:
        movable = [i for i in range(1, number_of) if counts[i] < largest] or [i for i in range(1, number_of) if counts[i] < bound]
        pool, budget = sum([loads[i] for i in movable]), surplus
        for i in movable:
            more = min(bound - counts[i], max(1, budget * loads[i] // pool), surplus)
            counts[i] = counts[i] + more
            surplus = surplus - more
    return np.array(counts)


def noise(stream_key, shape, deviation, bound, cuts=(), kind=jnp.bfloat16):
    entries = jax.random.normal(stream_key, shape, jnp.float32) * deviation
    if len(cuts) > 0:
        entries = steps_of(stream_key, shape, cuts, -0.22, 0.18) * entries
    return jnp.clip(entries, min=-bound, max=bound).astype(kind)


def setup_inputs(seed: int = 0) -> dict:
    seeds = jax.random.split(jax.random.key(seed), 11)
    q_nope = draw_q_nope(jax.random.fold_in(seeds[10], 71), 0)
    q_rope = noise(seeds[1], (REQS, STEPS, HEADS * ROPE), 1.0, 6.0, ((0, 32), (2, 8)))
    new_latent = noise(seeds[2], (REQS, STEPS, LAT), 1.0, 6.0, ((0, 32),))
    new_rope = noise(seeds[3], (REQS, STEPS, ROPE), 1.0, 6.0, ((0, 32),))
    pool_latent = noise(seeds[4], (POOLS, BLK, LAT), 1.0, 6.0, ((0, 32), (1, 8)))
    pool_rope = noise(seeds[5], (POOLS, BLK * ROPE), 1.0, 6.0, ((0, 32), (1, 8)))
    kv_weight = noise(seeds[6], (LAT, HEADS, NOPE + DV), LAT ** -0.5, 0.25, ((0, 32), (1, 8)))
    src_dev_keys = jax.random.split(jax.random.fold_in(seeds[7], 1), (REQS * MAXB) // (REQ_DEV * MAXB))
    src_dev_turns = jax.random.permutation(jax.random.fold_in(seeds[7], 3), (REQS * MAXB) // (REQ_DEV * MAXB))
    src_dev = jax.vmap(lambda own, number: shared_out(jax.random.fold_in(seeds[7], 2), own, number, REQ_DEV * MAXB, N_DP, 1, CAP, 1))(src_dev_keys, src_dev_turns).reshape((REQS * MAXB, 1))
    src_block = place_ends(jax.random.randint(seeds[8], (REQS * MAXB,), 0, POOL_DEV), jax.random.fold_in(seeds[8], 1), 0, POOL_DEV - 1).astype(jnp.int32)
    lengths = draw_lengths(jax.random.fold_in(seeds[10], 71), 0)
    return {"q_nope": q_nope, "q_rope": q_rope, "new_latent": new_latent, "new_rope": new_rope, "pool_latent": pool_latent, "pool_rope": pool_rope, "kv_weight": kv_weight, "src_dev": src_dev, "src_block": src_block, "lengths": lengths}


def rotate(values, positions):
    half = values.shape[-1] // 2
    freqs = 10000.0 ** (-(2.0 * jnp.arange(half, dtype=jnp.float32)) / (2.0 * half))
    angles = positions[..., None] * freqs
    first = values[..., :half]
    second = values[..., half:]
    cosine = jnp.cos(angles)
    sine = jnp.sin(angles)
    return jnp.concatenate([first * cosine - second * sine, first * sine + second * cosine], axis=-1)


def reference(q_nope, q_rope, new_latent, new_rope, pool_latent, pool_rope, kv_weight, src_dev, src_block, lengths):
    w_key = kv_weight[:, :, :NOPE].astype(jnp.float32)
    w_val = kv_weight[:, :, NOPE:].astype(jnp.float32)
    scale = (NOPE + ROPE) ** -0.5
    tables = (src_dev[:, 0] * POOL_DEV + src_block).astype(jnp.int32).reshape(REQS, MAXB)
    tokens = MAXB * BLK

    def single(items):
        query_n, query_r, lat_new, rope_new, table, length = items
        q_lat = jnp.einsum('shn,lhn->shl', query_n.reshape(STEPS, HEADS, NOPE).astype(jnp.float32), w_key).astype(jnp.bfloat16)
        positions = (length + jnp.arange(STEPS, dtype=jnp.int32)).astype(jnp.float32)
        q_rot = rotate(query_r.reshape(STEPS, HEADS, ROPE).astype(jnp.float32), positions[:, None]).astype(jnp.bfloat16)
        k_new = rotate(rope_new.astype(jnp.float32), positions).astype(jnp.bfloat16)
        cache_lat = pool_latent[table].reshape(tokens, LAT).astype(jnp.float32)
        cache_rope = pool_rope[table].reshape(tokens, ROPE).astype(jnp.float32)
        ql = q_lat.astype(jnp.float32)
        qr = q_rot.astype(jnp.float32)
        lat_f = lat_new.astype(jnp.float32)
        cached = jnp.einsum('shl,tl->sht', ql, cache_lat) + jnp.einsum('she,te->sht', qr, cache_rope)
        fresh = jnp.einsum('shl,ul->shu', ql, lat_f) + jnp.einsum('she,ue->shu', qr, k_new.astype(jnp.float32))
        scores = jnp.concatenate([cached, fresh], axis=-1) * scale
        valid_old = jnp.broadcast_to(jnp.arange(tokens, dtype=jnp.int32)[None, :] < length, (STEPS, tokens))
        valid_new = jnp.arange(STEPS, dtype=jnp.int32)[None, :] <= jnp.arange(STEPS, dtype=jnp.int32)[:, None]
        valid = jnp.concatenate([valid_old, valid_new], axis=-1)[:, None, :]
        probs = jax.nn.softmax(jnp.where(valid, scores, -jnp.inf), axis=-1).astype(jnp.bfloat16).astype(jnp.float32)
        o_lat = jnp.einsum('sht,tl->shl', probs[..., :tokens], cache_lat) + jnp.einsum('shu,ul->shl', probs[..., tokens:], lat_f)
        o_lat = o_lat.astype(jnp.bfloat16).astype(jnp.float32)
        result = jnp.einsum('shl,lhv->shv', o_lat, w_val).astype(jnp.bfloat16)
        return result.reshape(STEPS, HEADS * DV)

    return lax.map(single, (q_nope, q_rope, new_latent, new_rope, tables, lengths))
```

```python
import jax
import jax.numpy as jnp
from jax import lax
from jax.experimental import pallas as pl
from jax.experimental.pallas import tpu as pltpu
from jax.sharding import PartitionSpec as P

LAT = 512
ROPE = 64
NOPE = 128
DV = 128
CAP = 5
NDP = 32
NH = 8
MESH = pl.DeviceIdType.MESH
F32 = jnp.float32
BF16 = jnp.bfloat16
SCALE = (NOPE + ROPE) ** (-0.5)


def rotate(values, positions):
    half = values.shape[-1] // 2
    freqs = 10000.0 ** (-(2.0 * jnp.arange(half, dtype=jnp.float32)) / (2.0 * half))
    angles = positions[..., None] * freqs
    first = values[..., :half]
    second = values[..., half:]
    cosine = jnp.cos(angles)
    sine = jnp.sin(angles)
    return jnp.concatenate(
        [first * cosine - second * sine, first * sine + second * cosine], axis=-1
    )


def remote(src, dst, send_sem, recv_sem, device):
    return pltpu.make_async_remote_copy(
        src_ref=src,
        dst_ref=dst,
        send_sem=send_sem,
        recv_sem=recv_sem,
        device_id=device,
        device_id_type=MESH,
    )


def dot_nt(a, b):
    return lax.dot_general(a, b, (((1,), (1,)), ((), ())), preferred_element_type=F32)


def dot_nn(a, b):
    return lax.dot_general(a, b, (((1,), (0,)), ((), ())), preferred_element_type=F32)


def kernel(
    req_ref, slot_ref, rtab_ref, len_ref, pool_ref, rope_ref, wk_ref, wv_ref, qn_ref, qr_ref,
    newl_ref, newr_ref, out_ref,
    reqv, reqs, slat, srope, rlat, rrope, rropef, clat, crope, kmat, kr, wkf, wvf,
    qsend, qmat, qrm, osend, oall,
    local_sem, req_ss, req_rs, lat_ss, lat_rs, rope_ss, rope_rs,
    wk_ss, wk_rs, wv_ss, wv_rs, q_ss, q_rs, qr_ss, qr_rs, c_ss, c_rs, cr_ss, cr_rs, o_ss, o_rs,
):
    me = lax.axis_index("dp")
    h = lax.axis_index("head")
    x, zh, c = me // 8, (me // 2) % 4, me % 2

    def dp_peer(o):
        return ((x + o // 8) % 4) * 8 + ((zh + (o // 2) % 4) % 4) * 2 + (c + o % 2) % 2

    def head_peer(k):
        return (h + k) % NH

    barrier = pltpu.get_barrier_semaphore()

    @pl.loop(1, NDP)
    def _(o):
        pl.semaphore_signal(barrier, inc=1, device_id=(dp_peer(o), h), device_id_type=MESH)

    @pl.loop(1, NH)
    def _(k):
        pl.semaphore_signal(barrier, inc=1, device_id=(me, head_peer(k)), device_id_type=MESH)

    pl.semaphore_wait(barrier, NDP - 1 + NH - 1)

    def req_copy(o):
        p = dp_peer(o)
        return remote(req_ref.at[p], reqv.at[me], req_ss.at[p], req_rs.at[me], (p, h))

    def req_arrival(o):
        p = dp_peer(o)
        return remote(req_ref.at[p], reqv.at[p], req_ss.at[p], req_rs.at[p], (p, h))

    @pl.loop(1, NDP)
    def _(o):
        req_copy(o).start()

    def z_copy(own, full, ss, rs, k):
        p = (x * 8 + ((zh + k) % 4) * 2 + c, h)
        return remote(own, full.at[x, zh, c], ss.at[k], rs.at[k], p)

    def z_arrival(own, full, ss, rs, k):
        z = (zh + 4 - k) % 4
        return remote(own, full.at[x, z, c], ss.at[k], rs.at[k], (x * 8 + z * 2 + c, h))

    def x_copy(full, ss, rs, k):
        p = (((x + k) % 4) * 8 + zh * 2 + c, h)
        return remote(full.at[x, :, c], full.at[x, :, c], ss.at[3 + k], rs.at[3 + k], p)

    def x_arrival(full, ss, rs, k):
        xx = (x + 4 - k) % 4
        return remote(
            full.at[xx, :, c], full.at[xx, :, c], ss.at[3 + k], rs.at[3 + k], (xx * 8 + zh * 2 + c, h)
        )

    def core_copy(full, ss, rs):
        p = (x * 8 + zh * 2 + (1 - c), h)
        return remote(full.at[:, :, c], full.at[:, :, c], ss.at[7], rs.at[7], p)

    def core_arrival(full, ss, rs):
        p = (x * 8 + zh * 2 + (1 - c), h)
        return remote(full.at[:, :, 1 - c], full.at[:, :, 1 - c], ss.at[7], rs.at[7], p)

    def z_stage(own, full, ss, rs, sem):
        pltpu.make_async_copy(own, full.at[x, zh, c], sem).start()
        for k in (1, 2, 3):
            z_copy(own, full, ss, rs, k).start()

    def x_stage(own, full, ss, rs, sem):
        pltpu.make_async_copy(own, full.at[x, zh, c], sem).wait()
        for k in (1, 2, 3):
            z_arrival(own, full, ss, rs, k).wait_recv()
        for k in (1, 2, 3):
            x_copy(full, ss, rs, k).start()

    def core_stage(full, ss, rs):
        for k in (1, 2, 3):
            x_arrival(full, ss, rs, k).wait_recv()
        core_copy(full, ss, rs).start()

    def weights_sent(own, full, ss, rs):
        for k in (1, 2, 3):
            z_copy(own, full, ss, rs, k).wait_send()
            x_copy(full, ss, rs, k).wait_send()
        core_copy(full, ss, rs).wait_send()

    z_stage(wk_ref, wkf, wk_ss, wk_rs, local_sem.at[0])

    reqv[pl.ds(me, 1)] = req_ref[pl.ds(me, 1)]

    @pl.loop(1, NDP)
    def _(o):
        req_arrival(o).wait_recv()

    to_smem = pltpu.make_async_copy(reqv, reqs, local_sem.at[1])
    to_smem.start()
    to_smem.wait()

    lane8 = lax.broadcasted_iota(jnp.int32, (8, 128), 1)

    def gather(d, lat_dst, rope_dst):
        ids = [reqs[d, 0, s] for s in range(CAP)]
        for s in range(CAP):
            lat_dst[CAP * d + s] = pool_ref[ids[s]]
        ropes = [rope_ref[ids[s]] for s in range(CAP)]
        rows = [
            jnp.where(lane8 < 64, ropes[0], ropes[1]),
            jnp.where(lane8 < 64, ropes[2], ropes[3]),
            ropes[4],
            jnp.zeros((8, 128), F32),
        ]
        rope_dst[d] = jnp.concatenate(rows, axis=0).astype(BF16)

    def lat_copy(p):
        part = pl.ds(CAP * p, CAP)
        mine = pl.ds(CAP * me, CAP)
        return remote(slat.at[part], rlat.at[mine], lat_ss.at[p], lat_rs.at[me], (p, h))

    def lat_arrival(p):
        part = pl.ds(CAP * p, CAP)
        return remote(slat.at[part], rlat.at[part], lat_ss.at[p], lat_rs.at[p], (p, h))

    def rope_copy(p):
        return remote(srope.at[p], rrope.at[me], rope_ss.at[p], rope_rs.at[me], (p, h))

    def rope_arrival(p):
        return remote(srope.at[p], rrope.at[p], rope_ss.at[p], rope_rs.at[p], (p, h))

    @pl.loop(1, NDP)
    def _(o):
        p = dp_peer(o)
        gather(p, slat, srope)
        lat_copy(p).start()
        rope_copy(p).start()

    gather(me, rlat, rrope)

    def qr_copy(k):
        p = head_peer(k)
        rows = pl.ds(h * 64, 64)
        return remote(qr_ref.at[p], qrm.at[rows], qr_ss.at[k], qr_rs.at[k], (me, p))

    def qr_arrival(k):
        p = (h + NH - k) % NH
        rows = pl.ds(p * 64, 64)
        return remote(qr_ref.at[p], qrm.at[rows], qr_ss.at[k], qr_rs.at[k], (me, p))

    for k in range(1, NH):
        qr_copy(k).start()
    qr_own = pltpu.make_async_copy(qr_ref.at[h], qrm.at[pl.ds(h * 64, 64)], local_sem.at[2])
    qr_own.start()

    x_stage(wk_ref, wkf, wk_ss, wk_rs, local_sem.at[0])
    z_stage(wv_ref, wvf, wv_ss, wv_rs, local_sem.at[3])
    core_stage(wkf, wk_ss, wk_rs)
    core_arrival(wkf, wk_ss, wk_rs).wait_recv()

    sub8 = lax.broadcasted_iota(jnp.int32, (4, 8, LAT), 1)
    for quad in range(4):
        even, odd = [], []
        for pair in range(2):
            tiles = []
            for one in range(2):
                g = quad * 4 + pair * 2 + one
                weight = wkf[:, :, :, g].reshape(LAT, NOPE)
                tiles.append(dot_nt(qn_ref[:, g * NOPE : (g + 1) * NOPE], weight).reshape(4, 8, LAT))
            a, b = tiles
            even.append(jnp.where(sub8 < 4, a, pltpu.roll(b, 4, 1)))
            odd.append(jnp.where(sub8 < 4, pltpu.roll(a, 4, 1), b))
        rows = pl.ds(quad * 16, 16)
        qsend[:, 0, rows, :] = jnp.concatenate(even, axis=1).astype(BF16)
        qsend[:, 1, rows, :] = jnp.concatenate(odd, axis=1).astype(BF16)

    def q_copy(k):
        p = head_peer(k)
        rows = pl.ds(h * 64, 64)
        return remote(qsend.at[p // 2, p % 2], qmat.at[rows], q_ss.at[k], q_rs.at[k], (me, p))

    def q_arrival(k):
        p = (h + NH - k) % NH
        rows = pl.ds(p * 64, 64)
        return remote(qsend.at[p // 2, p % 2], qmat.at[rows], q_ss.at[k], q_rs.at[k], (me, p))

    for k in range(1, NH):
        q_copy(k).start()
    q_own = pltpu.make_async_copy(
        qsend.at[h // 2, h % 2], qmat.at[pl.ds(h * 64, 64)], local_sem.at[4]
    )
    q_own.start()

    x_stage(wv_ref, wvf, wv_ss, wv_rs, local_sem.at[3])
    core_stage(wvf, wv_ss, wv_rs)

    @pl.loop(1, NDP)
    def _(o):
        p = dp_peer(o)
        lat_arrival(p).wait_recv()
        rope_arrival(p).wait_recv()

    @pl.loop(0, NDP)
    def _(d):
        rropef[pl.ds(4 * d, 4)] = rrope[d].astype(F32).reshape(4, 8, 128)

    def c_copy(r, k):
        rows = pl.ds(h * 64, 64)
        return remote(clat.at[r], kmat.at[:, rows], c_ss.at[k], c_rs.at[k], (me, r))

    def c_arrival(k):
        p = (h + NH - k) % NH
        rows = pl.ds(p * 64, 64)
        return remote(clat.at[p], kmat.at[:, rows], c_ss.at[k], c_rs.at[k], (me, p))

    def cr_copy(r, k):
        rows = pl.ds(h * 64, 64)
        return remote(crope.at[r], kr.at[rows], cr_ss.at[k], cr_rs.at[k], (me, r))

    def cr_arrival(k):
        p = (h + NH - k) % NH
        rows = pl.ds(p * 64, 64)
        return remote(crope.at[p], kr.at[rows], cr_ss.at[k], cr_rs.at[k], (me, p))

    def side(entry, want):
        code = rtab_ref[entry]
        value = rropef[code // 2]
        turn = jnp.full((8, 128), code % 2, jnp.int32) != want
        return jnp.where(turn, pltpu.roll(value, 64, 1), value)

    def compact(r):
        for quarter in range(4):
            rows = pl.ds(quarter * 16, 16)
            for b in range(2):
                entry = r * 16 + b * 8 + quarter * 2
                first = rlat[slot_ref[entry]].astype(F32)
                second = rlat[slot_ref[entry + 1]].astype(F32)
                for j in range(4):
                    tile = jnp.concatenate(
                        [first[8 * j : 8 * j + 8], second[8 * j : 8 * j + 8]], axis=0
                    )
                    clat[r, b, rows, 128 * j : 128 * j + 128] = tile.astype(BF16)
            ropes = []
            for one in range(2):
                entry = r * 16 + quarter * 2 + one
                ropes.append(jnp.where(lane8 < 64, side(entry, 0), side(entry + 8, 1)))
            crope[r, rows, :] = jnp.concatenate(ropes, axis=0).astype(BF16)

    @pl.loop(1, NH)
    def _(k):
        r = head_peer(k)
        compact(r)
        c_copy(r, k).start()
        cr_copy(r, k).start()

    compact(h)
    own_rows = pl.ds(h * 64, 64)
    c_own = pltpu.make_async_copy(clat.at[h], kmat.at[:, own_rows], local_sem.at[5])
    cr_own = pltpu.make_async_copy(crope.at[h], kr.at[own_rows], local_sem.at[6])
    c_own.start()
    cr_own.start()

    qr_own.wait()
    q_own.wait()
    for k in range(1, NH):
        qr_arrival(k).wait_recv()
        q_arrival(k).wait_recv()
    c_own.wait()
    cr_own.wait()
    for k in range(1, NH):
        c_arrival(k).wait_recv()
        cr_arrival(k).wait_recv()

    length = len_ref[h]
    newl = jnp.concatenate([newl_ref[h], jnp.zeros((112, LAT), BF16)], axis=0)
    newr = jnp.concatenate([newr_ref[h], jnp.zeros((112, 128), BF16)], axis=0)
    column = lax.broadcasted_iota(jnp.int32, (1, 512), 1)
    token0 = ((column // 8) % 8) * 64 + (column // 64) * 8 + column % 8
    neg = -jnp.inf

    def o_copy(p, k):
        return remote(osend.at[pl.ds(p * 64, 64)], oall.at[h], o_ss.at[k], o_rs.at[k], (me, p))

    def o_arrival(k):
        p = (h + NH - k) % NH
        return remote(osend.at[pl.ds(p * 64, 64)], oall.at[p], o_ss.at[k], o_rs.at[k], (me, p))

    def attend(block):
        rows = pl.ds(pl.multiple_of(block * 128, 128), 128)
        q = qmat[rows, :]
        qrot = qrm[rows, :]
        turned = pltpu.roll(qrot.astype(F32), 64, 1).astype(BF16)
        s0 = (dot_nt(q, kmat[0]) + dot_nt(qrot, kr[...])) * SCALE
        s1 = (dot_nt(q, kmat[1]) + dot_nt(turned, kr[...])) * SCALE
        s2 = (dot_nt(q, newl) + dot_nt(qrot, newr)) * SCALE
        s0 = jnp.where(token0 < length, s0, neg)
        s1 = jnp.where(token0 + 512 < length, s1, neg)
        step = lax.broadcasted_iota(jnp.int32, (128, 128), 0) % 4
        s2 = jnp.where(lax.broadcasted_iota(jnp.int32, (128, 128), 1) <= step, s2, neg)
        top = jnp.maximum(
            jnp.maximum(jnp.max(s0, axis=1, keepdims=True), jnp.max(s1, axis=1, keepdims=True)),
            jnp.max(s2, axis=1, keepdims=True),
        )
        e0, e1, e2 = jnp.exp(s0 - top), jnp.exp(s1 - top), jnp.exp(s2 - top)
        total = (
            jnp.sum(e0, axis=1, keepdims=True)
            + jnp.sum(e1, axis=1, keepdims=True)
            + jnp.sum(e2, axis=1, keepdims=True)
        )
        inv = 1.0 / total
        o = dot_nn((e0 * inv).astype(BF16), kmat[0])
        o = o + dot_nn((e1 * inv).astype(BF16), kmat[1])
        o = o + dot_nn((e2 * inv).astype(BF16), newl)
        osend[rows, :] = o.astype(BF16)

    @pl.loop(1, 4)
    def _(i):
        block = (h // 2 + i) % 4
        attend(block)
        for one in range(2):
            p = 2 * block + one
            o_copy(p, (p + NH - h) % NH).start()

    attend(h // 2)
    partner = 2 * (h // 2) + 1 - h % 2
    o_copy(partner, (partner + NH - h) % NH).start()
    oall[pl.ds(h, 1)] = osend[pl.ds(pl.multiple_of(h * 64, 64), 64), :].reshape(1, 64, LAT)

    core_arrival(wvf, wv_ss, wv_rs).wait_recv()
    for k in range(1, NH):
        o_arrival(k).wait_recv()

    for quad in range(4):
        rows = pl.ds(quad * 16, 16)
        o_rows = oall[:, rows, :].astype(F32).reshape(4, 2, 16, LAT)
        for pair in range(2):
            even = o_rows[:, 0, pair * 8 : pair * 8 + 8]
            odd = o_rows[:, 1, pair * 8 : pair * 8 + 8]
            a = jnp.where(sub8 < 4, even, pltpu.roll(odd, 4, 1))
            b = jnp.where(sub8 < 4, pltpu.roll(even, 4, 1), odd)
            for one, value in enumerate((a, b)):
                g = quad * 4 + pair * 2 + one
                weight = wvf[:, :, :, g].reshape(LAT, DV)
                result = dot_nn(value.reshape(32, LAT).astype(BF16), weight)
                out_ref[:, g * DV : (g + 1) * DV] = result.astype(BF16)

    @pl.loop(1, NDP)
    def _(o):
        p = dp_peer(o)
        req_copy(o).wait_send()
        lat_copy(p).wait_send()
        rope_copy(p).wait_send()

    weights_sent(wk_ref, wkf, wk_ss, wk_rs)
    weights_sent(wv_ref, wvf, wv_ss, wv_rs)
    for k in range(1, NH):
        qr_copy(k).wait_send()
        q_copy(k).wait_send()
        c_copy(head_peer(k), k).wait_send()
        cr_copy(head_peer(k), k).wait_send()
        o_copy(head_peer(k), k).wait_send()


def per_device(
    q_nope,
    q_rope,
    new_latent,
    new_rope,
    pool_latent,
    pool_rope,
    kv_weight,
    src_dev,
    src_block,
    lengths,
):
    entries = src_block.shape[0]
    dev = src_dev[:, 0]
    ids = jnp.arange(entries, dtype=jnp.int32)
    same = (dev[:, None] == dev[None, :]) & (ids[:, None] < ids[None, :])
    rank = jnp.sum(same.astype(jnp.int32), axis=0)
    slots = dev * CAP + rank
    rtab = dev * 8 + rank
    lanes = jnp.arange(128, dtype=jnp.int32)
    code = jnp.arange(NDP, dtype=jnp.int32)[:, None] * 128 + lanes[None, :]
    hit = code[:, :, None] == (dev * 128 + rank)[None, None, :]
    req = jnp.sum(jnp.where(hit, src_block[None, None, :], 0), axis=2).reshape(NDP, 1, 128)

    blocks = pool_latent.shape[0]
    pool = pool_latent.reshape(blocks, 8, 4, 128).transpose(0, 2, 1, 3).reshape(blocks, 32, 128)
    rope = pool_rope.reshape(blocks, 8, ROPE).astype(F32)
    rope = jnp.concatenate([rope, rope], axis=-1)
    weight = kv_weight.transpose(1, 0, 2)
    wk, wv = weight[:, :, :NOPE], weight[:, :, NOPE:]

    requests, steps = q_nope.shape[0], q_nope.shape[1]
    positions = (lengths[:, None] + jnp.arange(steps, dtype=jnp.int32)[None, :]).astype(F32)
    q_rot = rotate(
        q_rope.reshape(requests, steps, 16, ROPE).astype(F32), positions[:, :, None]
    ).astype(BF16)
    q_rot = q_rot.transpose(0, 2, 1, 3).reshape(requests, 64, ROPE)
    q_rot = jnp.pad(q_rot, ((0, 0), (0, 0), (0, 128 - ROPE)))
    k_new = rotate(new_rope.astype(F32), positions).astype(BF16)
    k_new = jnp.pad(k_new, ((0, 0), (0, 16 - steps), (0, 128 - ROPE)))
    new_lat = jnp.pad(new_latent, ((0, 0), (0, 16 - steps), (0, 0)))
    qn = q_nope.reshape(requests * steps, 16 * NOPE)

    vm = pl.BlockSpec(memory_space=pltpu.VMEM)
    sm = pl.BlockSpec(memory_space=pltpu.SMEM)
    dma = pltpu.SemaphoreType.DMA
    out = pl.pallas_call(
        kernel,
        out_shape=jax.ShapeDtypeStruct((requests * steps, 16 * DV), BF16),
        in_specs=[vm, sm, sm, sm, vm, vm, vm, vm, vm, vm, vm, vm],
        out_specs=vm,
        scratch_shapes=[
            pltpu.VMEM((NDP, 1, 128), jnp.int32),
            pltpu.SMEM((NDP, 1, 128), jnp.int32),
            pltpu.VMEM((NDP * CAP, 32, 128), BF16),
            pltpu.VMEM((NDP, 32, 128), BF16),
            pltpu.VMEM((NDP * CAP, 32, 128), BF16),
            pltpu.VMEM((NDP, 32, 128), BF16),
            pltpu.VMEM((NDP * 4, 8, 128), F32),
            pltpu.VMEM((NH, 2, 64, LAT), BF16),
            pltpu.VMEM((NH, 64, 128), BF16),
            pltpu.VMEM((2, 512, LAT), BF16),
            pltpu.VMEM((512, 128), BF16),
            pltpu.VMEM((4, 4, 2, 16, 16, 128), BF16),
            pltpu.VMEM((4, 4, 2, 16, 16, 128), BF16),
            pltpu.VMEM((4, 2, 64, LAT), BF16),
            pltpu.VMEM((512, LAT), BF16),
            pltpu.VMEM((512, 128), BF16),
            pltpu.VMEM((512, LAT), BF16),
            pltpu.VMEM((NH, 64, LAT), BF16),
            dma((7,)),
            dma((NDP,)), dma((NDP,)), dma((NDP,)), dma((NDP,)), dma((NDP,)), dma((NDP,)),
            dma((8,)), dma((8,)), dma((8,)), dma((8,)),
            dma((NH,)), dma((NH,)), dma((NH,)), dma((NH,)), dma((NH,)), dma((NH,)),
            dma((NH,)), dma((NH,)), dma((NH,)), dma((NH,)),
        ],
        compiler_params=pltpu.CompilerParams(
            collective_id=0, has_side_effects=True, vmem_limit_bytes=48 << 20
        ),
    )(req, slots, rtab, lengths, pool, rope, wk, wv, qn, q_rot, new_lat, k_new)
    return out.reshape(requests, steps, 16 * DV)


def solution(mesh):
    in_specs = (
        P("dp", None, "head"),
        P("dp", None, "head"),
        P("dp", None, None),
        P("dp", None, None),
        P("dp", "head", None),
        P("dp", "head"),
        P("dp", "head", None),
        P("dp", None),
        P("dp"),
        P("dp"),
    )
    out_specs = P("dp", None, "head")
    return jax.shard_map(
        per_device, mesh=mesh, in_specs=in_specs, out_specs=out_specs, check_vma=False
    )
```

```python
import jax
import jax.numpy as jnp
import numpy as np
from jax import lax
from jax.experimental import pallas as pl
from jax.experimental.pallas import tpu as pltpu
from jax.sharding import PartitionSpec as P

LAT = 512
ROPE = 64
NOPE = 128
DV = 128
CAP = 5
NDP = 32
NH = 8
MESH = pl.DeviceIdType.MESH
F32 = jnp.float32
BF16 = jnp.bfloat16
SCALE = (NOPE + ROPE) ** (-0.5)
OTHERS = (0, 1, 2, 3, 5, 6, 7)


FREQS = np.tile(10000.0 ** (-(2.0 * np.arange(32)) / 64.0), 4).astype(np.float32).reshape(1, 128)


def rotated(values, cosine, sine):
    lane = lax.broadcasted_iota(jnp.int32, values.shape, 1) % 64
    ahead = pltpu.roll(values, 96, 1)
    behind = pltpu.roll(values, 32, 1)
    return values * cosine + jnp.where(lane < 32, -ahead, behind) * sine


def remote(src, dst, send_sem, recv_sem, device):
    return pltpu.make_async_remote_copy(
        src_ref=src,
        dst_ref=dst,
        send_sem=send_sem,
        recv_sem=recv_sem,
        device_id=device,
        device_id_type=MESH,
    )


def dot_nt(a, b):
    return lax.dot_general(a, b, (((1,), (1,)), ((), ())), preferred_element_type=F32)


def dot_nn(a, b):
    return lax.dot_general(a, b, (((1,), (0,)), ((), ())), preferred_element_type=F32)


def kernel(
    dev_ref, block_ref, len_ref, freq_ref, pool_hbm, rope_hbm, kv_hbm, qn_hbm, qr_hbm,
    newl_ref, newr_ref, out_ref,
    pool_ref, rope_ref, kv_ref, kvf, wk_ref, wv_ref, qn_ref, qr_ref, fetch_sem,
    req, tab, tabs, reqv, reqs, slat, srope, rlat, rrope, rropef, clat, crope, kmat, kr, wkf, wvf,
    qsend, qmat, osend, oall,
    local_sem, req_ss, req_rs, lat_ss, lat_rs, rope_ss, rope_rs,
    wk_ss, wk_rs, wv_ss, wv_rs, q_ss, q_rs, c_ss, c_rs, cr_ss, cr_rs, o_ss, o_rs,
):
    me = lax.axis_index("dp")
    h = lax.axis_index("head")
    x, zh, c = me // 8, (me // 2) % 4, me % 2

    def dp_peer(o):
        return ((x + o // 8) % 4) * 8 + ((zh + (o // 2) % 4) % 4) * 2 + (c + o % 2) % 2

    zl, y = h // 4, h % 4
    flip = (1 - zl) * 4 + y

    def across(o):
        return jnp.where((o // 2) % 4 == 2, flip, h)

    def head_peer(k):
        return ((zl + 1 + k // 4) % 2) * 4 + (y + k) % 4

    def head_from(k):
        return ((zl + 1 + k // 4) % 2) * 4 + (y + 4 - k % 4) % 4

    fetches = []
    for source, target in (
        (kv_hbm, kv_ref), (qr_hbm, qr_ref), (pool_hbm, pool_ref), (rope_hbm, rope_ref), (qn_hbm, qn_ref)
    ):
        fetches.append(pltpu.make_async_copy(source, target, fetch_sem.at[len(fetches)]))

    barrier = pltpu.get_barrier_semaphore()

    @pl.loop(1, NDP)
    def _(o):
        pl.semaphore_signal(
            barrier, inc=1, device_id=(dp_peer(o), across(o)), device_id_type=MESH
        )

    for k in OTHERS:
        pl.semaphore_signal(barrier, inc=1, device_id=(me, head_peer(k)), device_id_type=MESH)

    for fetch in fetches:
        fetch.start()

    dev = dev_ref[...]
    blk = block_ref[...]
    row = lax.broadcasted_iota(jnp.int32, (128, 128), 0)
    col = lax.broadcasted_iota(jnp.int32, (128, 128), 1)
    dev_rows = jnp.broadcast_to(dev, (128, 128))
    dev_col = jnp.sum(jnp.where(row == col, dev_rows, 0), axis=1, keepdims=True)
    same = jnp.where((dev_col == dev_rows) & (row < col), 1, 0)
    rank = jnp.sum(same, axis=0, keepdims=True)
    source = lax.broadcasted_iota(jnp.int32, (NDP, 128), 0)
    lanes = lax.broadcasted_iota(jnp.int32, (NDP, 128), 1)
    asked = jnp.zeros((NDP, 128), jnp.int32)
    for slot in range(CAP):
        hit = (source == dev) & (rank == slot)
        found = jnp.sum(jnp.where(hit, blk, 0), axis=1, keepdims=True)
        asked = jnp.where(lanes == slot, found, asked)
    req[...] = asked.reshape(NDP, 1, 128)
    tab[0:1, :] = dev * CAP + rank
    tab[1:2, :] = dev * 8 + rank
    tab_copy = pltpu.make_async_copy(tab, tabs, local_sem.at[2])
    tab_copy.start()

    fetches[0].wait()
    kvf[...] = kv_ref[...].astype(F32)
    for g in range(16):
        one_head = kvf[:, g, :]
        wk_ref[g] = one_head[:, :NOPE].astype(BF16)
        wv_ref[g] = one_head[:, NOPE:].astype(BF16)

    fetches[1].wait()
    low = lax.broadcasted_iota(jnp.int32, (32, 128), 1) < 64
    request = lax.broadcasted_iota(jnp.int32, (32, 128), 0)
    position = request % 4
    for r in range(8):
        position = position + jnp.where(request // 4 == r, len_ref[r], 0)
    angle = position.astype(F32) * freq_ref[...]
    cosine, sine = jnp.cos(angle), jnp.sin(angle)

    def by_request(tiles):
        width = tiles[0].shape[-1]
        first = lax.broadcasted_iota(jnp.int32, (4, 8, width), 1) < 4
        even, odd = [], []
        for pair in range(2):
            a = tiles[2 * pair].reshape(4, 8, width)
            b = tiles[2 * pair + 1].reshape(4, 8, width)
            even.append(jnp.where(first, a, pltpu.roll(b, 4, 1)))
            odd.append(jnp.where(first, pltpu.roll(a, 4, 1), b))
        return (
            jnp.concatenate(even, axis=1).astype(BF16),
            jnp.concatenate(odd, axis=1).astype(BF16),
        )

    for quad in range(4):
        tiles = []
        for pair in range(2):
            at = (quad * 2 + pair) * 128
            turned = rotated(qr_ref[:, at : at + 128].astype(F32), cosine, sine)
            tiles.append(jnp.where(low, turned, 0.0))
            tiles.append(jnp.where(low, pltpu.roll(turned, 64, 1), 0.0))
        even, odd = by_request(tiles)
        qsend[:, 0, quad * 16 : quad * 16 + 16, LAT:] = even
        qsend[:, 1, quad * 16 : quad * 16 + 16, LAT:] = odd

    pl.semaphore_wait(barrier, NDP - 1 + NH - 1)

    def req_copy(o):
        p = dp_peer(o)
        return remote(req.at[p], reqv.at[me], req_ss.at[p], req_rs.at[me], (p, across(o)))

    def req_arrival(o):
        p = dp_peer(o)
        return remote(req.at[p], reqv.at[p], req_ss.at[p], req_rs.at[p], (p, across(o)))

    def z_dev(k):
        return (x * 8 + ((zh + k) % 4) * 2 + c, h)

    def z_copy(own, full, ss, rs, k):
        return remote(own, full.at[x, zh, c], ss.at[k], rs.at[k], z_dev(k))

    def z_arrival(own, full, ss, rs, k):
        return remote(own, full.at[x, (zh + 4 - k) % 4, c], ss.at[k], rs.at[k], z_dev(k))

    def z_relay(full, ss, rs, k):
        part = full.at[x, (zh + 4 - k) % 4, c, pl.ds(0 if k == 1 else 8, 8)]
        return remote(part, part, ss.at[8 + k], rs.at[8 + k], z_dev(k))

    def z_relay_arrival(full, ss, rs, k):
        part = full.at[x, (zh + 2) % 4, c, pl.ds(0 if k == 1 else 8, 8)]
        return remote(part, part, ss.at[8 + k], rs.at[8 + k], z_dev(k))

    def x_copy(full, ss, rs, k):
        p = (((x + k) % 4) * 8 + zh * 2 + c, h)
        return remote(full.at[x, :, c], full.at[x, :, c], ss.at[3 + k], rs.at[3 + k], p)

    def x_arrival(full, ss, rs, k):
        xx = (x + 4 - k) % 4
        return remote(
            full.at[xx, :, c], full.at[xx, :, c], ss.at[3 + k], rs.at[3 + k], (xx * 8 + zh * 2 + c, h)
        )

    def core_copy(full, ss, rs):
        p = (x * 8 + zh * 2 + (1 - c), h)
        return remote(full.at[:, :, c], full.at[:, :, c], ss.at[7], rs.at[7], p)

    def core_arrival(full, ss, rs):
        p = (x * 8 + zh * 2 + (1 - c), h)
        return remote(full.at[:, :, 1 - c], full.at[:, :, 1 - c], ss.at[7], rs.at[7], p)

    def z_stage(own, full, ss, rs, sem):
        pltpu.make_async_copy(own, full.at[x, zh, c], sem).start()
        for k in (1, 3):
            z_copy(own, full, ss, rs, k).start()

    def z_pass(own, full, ss, rs):
        for k in (1, 3):
            z_arrival(own, full, ss, rs, k).wait_recv()
            z_relay(full, ss, rs, k).start()

    def x_stage(own, full, ss, rs, sem):
        pltpu.make_async_copy(own, full.at[x, zh, c], sem).wait()
        for k in (1, 3):
            z_relay_arrival(full, ss, rs, k).wait_recv()
        for k in (1, 2, 3):
            x_copy(full, ss, rs, k).start()

    def core_stage(full, ss, rs):
        for k in (1, 2, 3):
            x_arrival(full, ss, rs, k).wait_recv()
        core_copy(full, ss, rs).start()

    def weights_sent(own, full, ss, rs):
        for k in (1, 3):
            z_copy(own, full, ss, rs, k).wait_send()
            z_relay(full, ss, rs, k).wait_send()
        for k in (1, 2, 3):
            x_copy(full, ss, rs, k).wait_send()
        core_copy(full, ss, rs).wait_send()

    @pl.loop(1, NDP)
    def _(o):
        req_copy(o).start()

    z_stage(wk_ref, wkf, wk_ss, wk_rs, local_sem.at[0])
    z_stage(wv_ref, wvf, wv_ss, wv_rs, local_sem.at[3])
    reqv[pl.ds(me, 1)] = req[pl.ds(me, 1)]
    z_pass(wk_ref, wkf, wk_ss, wk_rs)
    z_pass(wv_ref, wvf, wv_ss, wv_rs)

    @pl.loop(1, NDP)
    def _(o):
        req_arrival(o).wait_recv()

    to_smem = pltpu.make_async_copy(reqv, reqs, local_sem.at[1])
    to_smem.start()
    to_smem.wait()
    x_stage(wk_ref, wkf, wk_ss, wk_rs, local_sem.at[0])
    fetches[2].wait()
    fetches[3].wait()

    lane8 = lax.broadcasted_iota(jnp.int32, (8, 128), 1)

    def gather(d, lat_dst, rope_dst):
        ids = [reqs[d, 0, s] for s in range(CAP)]
        for s in range(CAP):
            lat_dst[CAP * d + s] = pool_ref[ids[s]]
        ropes = [rope_ref[ids[s]] for s in range(CAP)]
        rows = [
            jnp.where(lane8 < 64, ropes[0], ropes[1]),
            jnp.where(lane8 < 64, ropes[2], ropes[3]),
            ropes[4],
            jnp.zeros((8, 128), F32),
        ]
        rope_dst[d] = jnp.concatenate(rows, axis=0).astype(BF16)

    def lat_copy(o):
        p = dp_peer(o)
        part = pl.ds(CAP * p, CAP)
        mine = pl.ds(CAP * me, CAP)
        return remote(slat.at[part], rlat.at[mine], lat_ss.at[p], lat_rs.at[me], (p, across(o)))

    def lat_arrival(o):
        p = dp_peer(o)
        part = pl.ds(CAP * p, CAP)
        return remote(slat.at[part], rlat.at[part], lat_ss.at[p], lat_rs.at[p], (p, across(o)))

    def rope_copy(o):
        p = dp_peer(o)
        return remote(srope.at[p], rrope.at[me], rope_ss.at[p], rope_rs.at[me], (p, across(o)))

    def rope_arrival(o):
        p = dp_peer(o)
        return remote(srope.at[p], rrope.at[p], rope_ss.at[p], rope_rs.at[p], (p, across(o)))

    @pl.loop(1, NDP)
    def _(o):
        gather(dp_peer(o), slat, srope)
        lat_copy(o).start()
        rope_copy(o).start()

    gather(me, rlat, rrope)

    core_stage(wkf, wk_ss, wk_rs)
    core_arrival(wkf, wk_ss, wk_rs).wait_recv()

    fetches[4].wait()

    for quad in range(4):
        tiles = []
        for g in range(quad * 4, quad * 4 + 4):
            weight = wkf[:, :, :, g].reshape(LAT, NOPE)
            tiles.append(dot_nt(qn_ref[:, g * NOPE : (g + 1) * NOPE], weight))
        even, odd = by_request(tiles)
        qsend[:, 0, quad * 16 : quad * 16 + 16, :LAT] = even
        qsend[:, 1, quad * 16 : quad * 16 + 16, :LAT] = odd

    def q_copy(k):
        p = head_peer(k)
        rows = pl.ds(h * 64, 64)
        return remote(qsend.at[p // 2, p % 2], qmat.at[rows], q_ss.at[k], q_rs.at[k], (me, p))

    def q_arrival(k):
        p = head_from(k)
        rows = pl.ds(p * 64, 64)
        return remote(qsend.at[p // 2, p % 2], qmat.at[rows], q_ss.at[k], q_rs.at[k], (me, p))

    for k in OTHERS:
        q_copy(k).start()
    q_own = pltpu.make_async_copy(
        qsend.at[h // 2, h % 2], qmat.at[pl.ds(h * 64, 64)], local_sem.at[4]
    )
    q_own.start()

    x_stage(wv_ref, wvf, wv_ss, wv_rs, local_sem.at[3])
    tab_copy.wait()

    @pl.loop(1, NDP)
    def _(o):
        lat_arrival(o).wait_recv()
        rope_arrival(o).wait_recv()

    @pl.loop(0, NDP)
    def _(d):
        rropef[pl.ds(4 * d, 4)] = rrope[d].astype(F32).reshape(4, 8, 128)

    def c_copy(r, k):
        rows = pl.ds(h * 64, 64)
        return remote(clat.at[r], kmat.at[:, rows], c_ss.at[k], c_rs.at[k], (me, r))

    def c_arrival(k):
        p = head_from(k)
        rows = pl.ds(p * 64, 64)
        return remote(clat.at[p], kmat.at[:, rows], c_ss.at[k], c_rs.at[k], (me, p))

    def cr_copy(r, k):
        rows = pl.ds(h * 64, 64)
        return remote(crope.at[r], kr.at[rows], cr_ss.at[k], cr_rs.at[k], (me, r))

    def cr_arrival(k):
        p = head_from(k)
        rows = pl.ds(p * 64, 64)
        return remote(crope.at[p], kr.at[rows], cr_ss.at[k], cr_rs.at[k], (me, p))

    def side(entry, want):
        code = tabs[1, entry]
        value = rropef[code // 2]
        turn = jnp.full((8, 128), code % 2, jnp.int32) != want
        return jnp.where(turn, pltpu.roll(value, 64, 1), value)

    def compact(r):
        for quarter in range(4):
            rows = pl.ds(quarter * 16, 16)
            for b in range(2):
                entry = r * 16 + b * 8 + quarter * 2
                first = rlat[tabs[0, entry]].astype(F32)
                second = rlat[tabs[0, entry + 1]].astype(F32)
                for j in range(4):
                    tile = jnp.concatenate(
                        [first[8 * j : 8 * j + 8], second[8 * j : 8 * j + 8]], axis=0
                    )
                    clat[r, b, rows, 128 * j : 128 * j + 128] = tile.astype(BF16)
            ropes = []
            for one in range(2):
                entry = r * 16 + quarter * 2 + one
                ropes.append(jnp.where(lane8 < 64, side(entry, 0), side(entry + 8, 1)))
            crope[r, rows, :] = jnp.concatenate(ropes, axis=0).astype(BF16)

    @pl.loop(0, NH)
    def _(k):
        @pl.when(k != 4)
        def _():
            r = head_peer(k)
            compact(r)
            c_copy(r, k).start()
            cr_copy(r, k).start()

    compact(h)
    own_rows = pl.ds(h * 64, 64)
    c_own = pltpu.make_async_copy(clat.at[h], kmat.at[:, own_rows], local_sem.at[5])
    cr_own = pltpu.make_async_copy(crope.at[h], kr.at[own_rows], local_sem.at[6])
    c_own.start()
    cr_own.start()
    core_stage(wvf, wv_ss, wv_rs)

    q_own.wait()
    for k in OTHERS:
        q_arrival(k).wait_recv()
    c_own.wait()
    cr_own.wait()
    for k in OTHERS:
        c_arrival(k).wait_recv()
        cr_arrival(k).wait_recv()

    length = len_ref[h]
    newl = jnp.concatenate([newl_ref[h], jnp.zeros((112, LAT), BF16)], axis=0)
    place = length + lax.broadcasted_iota(jnp.int32, (8, 128), 0)
    angle_new = place.astype(F32) * freq_ref[...]
    turned_new = rotated(newr_ref[h], jnp.cos(angle_new), jnp.sin(angle_new))
    newr = jnp.concatenate([turned_new, jnp.zeros((120, 128), F32)], axis=0).astype(BF16)
    column = lax.broadcasted_iota(jnp.int32, (1, 512), 1)
    of_entry = (column // 8) % 8
    tokens = []
    for b in range(2):
        moved = jnp.zeros((1, 512), jnp.int32)
        for e in range(8):
            code = tabs[1, h * 16 + b * 8 + e]
            far = (code // 16 + 4 - zh) % 4
            moved = jnp.where(of_entry == e, far, moved)
        part = jnp.where(moved == 2, (column // 64 + 4) % 8, column // 64)
        tokens.append((of_entry + 8 * b) * 64 + part * 8 + column % 8)
    neg = -jnp.inf

    def o_copy(p, k):
        return remote(osend.at[pl.ds(p * 64, 64)], oall.at[h], o_ss.at[k], o_rs.at[k], (me, p))

    def o_arrival(k):
        p = head_from(k)
        return remote(osend.at[pl.ds(p * 64, 64)], oall.at[p], o_ss.at[k], o_rs.at[k], (me, p))

    def step_to(p):
        return ((p // 4 + zl + 1) % 2) * 4 + (p + 4 - y) % 4

    def attend(block):
        rows = pl.ds(pl.multiple_of(block * 128, 128), 128)
        q = qmat[rows, :LAT]
        qrot = qmat[rows, LAT:]
        turned = pltpu.roll(qrot.astype(F32), 64, 1).astype(BF16)
        s0 = (dot_nt(q, kmat[0]) + dot_nt(qrot, kr[...])) * SCALE
        s1 = (dot_nt(q, kmat[1]) + dot_nt(turned, kr[...])) * SCALE
        s2 = (dot_nt(q, newl) + dot_nt(qrot, newr)) * SCALE
        s0 = jnp.where(tokens[0] < length, s0, neg)
        s1 = jnp.where(tokens[1] < length, s1, neg)
        step = lax.broadcasted_iota(jnp.int32, (128, 128), 0) % 4
        s2 = jnp.where(lax.broadcasted_iota(jnp.int32, (128, 128), 1) <= step, s2, neg)
        top = jnp.maximum(
            jnp.maximum(jnp.max(s0, axis=1, keepdims=True), jnp.max(s1, axis=1, keepdims=True)),
            jnp.max(s2, axis=1, keepdims=True),
        )
        e0, e1, e2 = jnp.exp(s0 - top), jnp.exp(s1 - top), jnp.exp(s2 - top)
        total = (
            jnp.sum(e0, axis=1, keepdims=True)
            + jnp.sum(e1, axis=1, keepdims=True)
            + jnp.sum(e2, axis=1, keepdims=True)
        )
        inv = 1.0 / total
        o = dot_nn((e0 * inv).astype(BF16), kmat[0])
        o = o + dot_nn((e1 * inv).astype(BF16), kmat[1])
        o = o + dot_nn((e2 * inv).astype(BF16), newl)
        osend[rows, :] = o.astype(BF16)

    @pl.loop(0, 3)
    def _(i):
        half = (zl + 1 + i // 2) % 2
        block = half * 2 + (y // 2 + (i + 1) // 2) % 2
        attend(block)
        for one in range(2):
            p = 2 * block + one
            o_copy(p, step_to(p)).start()

    attend(h // 2)
    partner = 2 * (h // 2) + 1 - h % 2
    o_copy(partner, step_to(partner)).start()
    oall[pl.ds(h, 1)] = osend[pl.ds(pl.multiple_of(h * 64, 64), 64), :].reshape(1, 64, LAT)

    core_arrival(wvf, wv_ss, wv_rs).wait_recv()
    for k in OTHERS:
        o_arrival(k).wait_recv()

    first4 = lax.broadcasted_iota(jnp.int32, (4, 8, LAT), 1) < 4
    for quad in range(4):
        rows = pl.ds(quad * 16, 16)
        o_rows = oall[:, rows, :].astype(F32).reshape(4, 2, 16, LAT)
        for pair in range(2):
            even = o_rows[:, 0, pair * 8 : pair * 8 + 8]
            odd = o_rows[:, 1, pair * 8 : pair * 8 + 8]
            a = jnp.where(first4, even, pltpu.roll(odd, 4, 1))
            b = jnp.where(first4, pltpu.roll(even, 4, 1), odd)
            for one, value in enumerate((a, b)):
                g = quad * 4 + pair * 2 + one
                weight = wvf[:, :, :, g].reshape(LAT, DV)
                result = dot_nn(value.reshape(32, LAT).astype(BF16), weight)
                out_ref[:, g * DV : (g + 1) * DV] = result.astype(BF16)

    @pl.loop(1, NDP)
    def _(o):
        req_copy(o).wait_send()
        lat_copy(o).wait_send()
        rope_copy(o).wait_send()

    weights_sent(wk_ref, wkf, wk_ss, wk_rs)
    weights_sent(wv_ref, wvf, wv_ss, wv_rs)
    for k in OTHERS:
        q_copy(k).wait_send()
        c_copy(head_peer(k), k).wait_send()
        cr_copy(head_peer(k), k).wait_send()
        o_copy(head_peer(k), k).wait_send()


def per_device(
    q_nope,
    q_rope,
    new_latent,
    new_rope,
    pool_latent,
    pool_rope,
    kv_weight,
    src_dev,
    src_block,
    lengths,
):
    blocks = pool_latent.shape[0]
    pool = pool_latent.reshape(blocks, 8, 4, 128).transpose(0, 2, 1, 3).reshape(blocks, 32, 128)
    rope = pool_rope.reshape(blocks, 8, ROPE).astype(F32)
    rope = jnp.concatenate([rope, rope], axis=-1)
    requests, steps = q_nope.shape[0], q_nope.shape[1]
    qr = q_rope.reshape(requests * steps, 16 * ROPE)
    new_rot = jnp.pad(new_rope.astype(F32), ((0, 0), (0, 8 - steps), (0, 128 - ROPE)))
    new_lat = jnp.pad(new_latent, ((0, 0), (0, 16 - steps), (0, 0)))
    qn = q_nope.reshape(requests * steps, 16 * NOPE)

    vm = pl.BlockSpec(memory_space=pltpu.VMEM)
    sm = pl.BlockSpec(memory_space=pltpu.SMEM)
    hbm = pl.BlockSpec(memory_space=pl.ANY)
    dma = pltpu.SemaphoreType.DMA
    out = pl.pallas_call(
        kernel,
        out_shape=jax.ShapeDtypeStruct((requests * steps, 16 * DV), BF16),
        in_specs=[vm, vm, sm, vm, hbm, hbm, hbm, hbm, hbm, vm, vm],
        out_specs=vm,
        scratch_shapes=[
            pltpu.VMEM((blocks, 32, 128), BF16),
            pltpu.VMEM((blocks, 8, 128), F32),
            pltpu.VMEM((16, 16, NOPE + DV), BF16),
            pltpu.VMEM((16, 16, NOPE + DV), F32),
            pltpu.VMEM((16, 16, NOPE), BF16),
            pltpu.VMEM((16, 16, DV), BF16),
            pltpu.VMEM((32, 16 * NOPE), BF16),
            pltpu.VMEM((32, 16 * ROPE), BF16),
            dma((5,)),
            pltpu.VMEM((NDP, 1, 128), jnp.int32),
            pltpu.VMEM((8, 128), jnp.int32),
            pltpu.SMEM((8, 128), jnp.int32),
            pltpu.VMEM((NDP, 1, 128), jnp.int32),
            pltpu.SMEM((NDP, 1, 128), jnp.int32),
            pltpu.VMEM((NDP * CAP, 32, 128), BF16),
            pltpu.VMEM((NDP, 32, 128), BF16),
            pltpu.VMEM((NDP * CAP, 32, 128), BF16),
            pltpu.VMEM((NDP, 32, 128), BF16),
            pltpu.VMEM((NDP * 4, 8, 128), F32),
            pltpu.VMEM((NH, 2, 64, LAT), BF16),
            pltpu.VMEM((NH, 64, 128), BF16),
            pltpu.VMEM((2, 512, LAT), BF16),
            pltpu.VMEM((512, 128), BF16),
            pltpu.VMEM((4, 4, 2, 16, 16, 128), BF16),
            pltpu.VMEM((4, 4, 2, 16, 16, 128), BF16),
            pltpu.VMEM((4, 2, 64, LAT + 128), BF16),
            pltpu.VMEM((512, LAT + 128), BF16),
            pltpu.VMEM((512, LAT), BF16),
            pltpu.VMEM((NH, 64, LAT), BF16),
            dma((7,)),
            dma((NDP,)), dma((NDP,)), dma((NDP,)), dma((NDP,)), dma((NDP,)), dma((NDP,)),
            dma((12,)), dma((12,)), dma((12,)), dma((12,)),
            dma((NH,)), dma((NH,)), dma((NH,)), dma((NH,)),
            dma((NH,)), dma((NH,)), dma((NH,)), dma((NH,)),
        ],
        compiler_params=pltpu.CompilerParams(
            collective_id=0, has_side_effects=True, vmem_limit_bytes=48 << 20
        ),
    )(
        src_dev.reshape(1, -1), src_block.reshape(1, -1), lengths, jnp.asarray(FREQS),
        pool, rope, kv_weight, qn, qr, new_lat, new_rot,
    )
    return out.reshape(requests, steps, 16 * DV)


def solution(mesh):
    in_specs = (
        P("dp", None, "head"),
        P("dp", None, "head"),
        P("dp", None, None),
        P("dp", None, None),
        P("dp", "head", None),
        P("dp", "head"),
        P("dp", "head", None),
        P("dp", None),
        P("dp"),
        P("dp"),
    )
    out_specs = P("dp", None, "head")
    return jax.shard_map(
        per_device, mesh=mesh, in_specs=in_specs, out_specs=out_specs, check_vma=False
    )
```

```python
import jax
import jax.numpy as jnp
import numpy as np
from jax import lax
from jax.experimental import pallas as pl
from jax.experimental.pallas import tpu as pltpu
from jax.sharding import PartitionSpec as P

LAT = 512
ROPE = 64
NOPE = 128
DV = 128
CAP = 5
PART = CAP + 1
NDP = 32
NH = 8
MESH = pl.DeviceIdType.MESH
F32 = jnp.float32
BF16 = jnp.bfloat16
SCALE = (NOPE + ROPE) ** (-0.5)
OTHERS = (0, 1, 2, 3, 5, 6, 7)


FREQS = np.tile(10000.0 ** (-(2.0 * np.arange(32)) / 64.0), 4).astype(np.float32).reshape(1, 128)


def rotated(values, cosine, sine):
    lane = lax.broadcasted_iota(jnp.int32, values.shape, 1) % 64
    ahead = pltpu.roll(values, 96, 1)
    behind = pltpu.roll(values, 32, 1)
    return values * cosine + jnp.where(lane < 32, -ahead, behind) * sine


def remote(src, dst, send_sem, recv_sem, device):
    return pltpu.make_async_remote_copy(
        src_ref=src,
        dst_ref=dst,
        send_sem=send_sem,
        recv_sem=recv_sem,
        device_id=device,
        device_id_type=MESH,
    )


def settle(like, sem):
    pltpu.make_async_copy(like, like, sem).wait()


def dot_nt(a, b):
    return lax.dot_general(a, b, (((1,), (1,)), ((), ())), preferred_element_type=F32)


def dot_nn(a, b):
    return lax.dot_general(a, b, (((1,), (0,)), ((), ())), preferred_element_type=F32)


def kernel(
    dev_ref, block_ref, len_ref, freq_ref, pool_hbm, rope_hbm, kv_hbm, qn_hbm, qr_hbm,
    newl_ref, newr_ref, out_ref,
    pool_ref, rope_ref, kv_ref, kvf, wk_ref, wv_ref, qn_ref, qr_ref, fetch_sem,
    req, tab, tabs, reqv, reqs, slat, rlat0, rlat1, rropef, clat, crope, kmat, kr, wkf, wvf,
    qsend, qmat, osend, oall,
    local_sem, req_s, req_r, lat_s, lat_r, wk_ss, wk_rs, wv_ss, wv_rs,
    q_s, q_r, c_s, c_r, cr_s, cr_r, o_s, o_r,
):
    rlat = (rlat0, rlat1)
    me = lax.axis_index("dp")
    h = lax.axis_index("head")
    x, zh, c = me // 8, (me // 2) % 4, me % 2

    def dp_peer(o):
        return ((x + 4 - o // 8) % 4) * 8 + ((zh + 4 - (o // 2) % 4) % 4) * 2 + (c + o % 2) % 2

    zl, y = h // 4, h % 4
    flip = (1 - zl) * 4 + y

    def across(o):
        return jnp.where((o // 2) % 4 == 2, flip, h)

    def head_peer(k):
        return ((zl + 1 + k // 4) % 2) * 4 + (y + k) % 4

    def head_from(k):
        return ((zl + 1 + k // 4) % 2) * 4 + (y + 4 - k % 4) % 4

    fetches = []
    for source, target in (
        (kv_hbm, kv_ref), (qr_hbm, qr_ref), (pool_hbm, pool_ref), (rope_hbm, rope_ref), (qn_hbm, qn_ref)
    ):
        fetches.append(pltpu.make_async_copy(source, target, fetch_sem.at[len(fetches)]))

    barrier = pltpu.get_barrier_semaphore()

    @pl.loop(1, NDP)
    def _(o):
        pl.semaphore_signal(
            barrier, inc=1, device_id=(dp_peer(o), across(o)), device_id_type=MESH
        )

    for k in OTHERS:
        pl.semaphore_signal(barrier, inc=1, device_id=(me, head_peer(k)), device_id_type=MESH)

    for fetch in fetches:
        fetch.start()

    dev = dev_ref[...]
    blk = block_ref[...]
    row = lax.broadcasted_iota(jnp.int32, (128, 128), 0)
    col = lax.broadcasted_iota(jnp.int32, (128, 128), 1)
    dev_rows = jnp.broadcast_to(dev, (128, 128))
    dev_col = jnp.sum(jnp.where(row == col, dev_rows, 0), axis=1, keepdims=True)
    same = jnp.where((dev_col == dev_rows) & (row < col), 1, 0)
    rank = jnp.sum(same, axis=0, keepdims=True)
    source = lax.broadcasted_iota(jnp.int32, (NDP, 128), 0)
    lanes = lax.broadcasted_iota(jnp.int32, (NDP, 128), 1)
    asked = jnp.zeros((NDP, 128), jnp.int32)
    for slot in range(CAP):
        hit = (source == dev) & (rank == slot)
        found = jnp.sum(jnp.where(hit, blk, 0), axis=1, keepdims=True)
        asked = jnp.where(lanes == slot, found, asked)
    req[...] = asked.reshape(NDP, 1, 128)
    tab[0:1, :] = dev * PART + rank
    tab[1:2, :] = dev * 8 + rank
    tab_copy = pltpu.make_async_copy(tab, tabs, local_sem.at[2])
    tab_copy.start()

    fetches[0].wait()
    kvf[...] = kv_ref[...].astype(F32)
    for g in range(16):
        one_head = kvf[:, g, :]
        wk_ref[g] = one_head[:, :NOPE].astype(BF16)
        wv_ref[g] = one_head[:, NOPE:].astype(BF16)

    fetches[1].wait()
    low = lax.broadcasted_iota(jnp.int32, (32, 128), 1) < 64
    request = lax.broadcasted_iota(jnp.int32, (32, 128), 0)
    position = request % 4
    for r in range(8):
        position = position + jnp.where(request // 4 == r, len_ref[r], 0)
    angle = position.astype(F32) * freq_ref[...]
    cosine, sine = jnp.cos(angle), jnp.sin(angle)

    def by_request(tiles):
        width = tiles[0].shape[-1]
        first = lax.broadcasted_iota(jnp.int32, (4, 8, width), 1) < 4
        even, odd = [], []
        for pair in range(2):
            a = tiles[2 * pair].reshape(4, 8, width)
            b = tiles[2 * pair + 1].reshape(4, 8, width)
            even.append(jnp.where(first, a, pltpu.roll(b, 4, 1)))
            odd.append(jnp.where(first, pltpu.roll(a, 4, 1), b))
        return (
            jnp.concatenate(even, axis=1).astype(BF16),
            jnp.concatenate(odd, axis=1).astype(BF16),
        )

    for quad in range(4):
        tiles = []
        for pair in range(2):
            at = (quad * 2 + pair) * 128
            turned = rotated(qr_ref[:, at : at + 128].astype(F32), cosine, sine)
            tiles.append(jnp.where(low, turned, 0.0))
            tiles.append(jnp.where(low, pltpu.roll(turned, 64, 1), 0.0))
        even, odd = by_request(tiles)
        qsend[:, 0, quad * 16 : quad * 16 + 16, LAT:] = even
        qsend[:, 1, quad * 16 : quad * 16 + 16, LAT:] = odd

    pl.semaphore_wait(barrier, NDP - 1 + NH - 1)

    def req_copy(o):
        p = dp_peer(o)
        return remote(req.at[p], reqv.at[me], req_s, req_r, (p, across(o)))

    def along_z(k):
        return (x * 8 + ((zh + k) % 4) * 2 + c, h)

    def along_x(k):
        return (((x + k) % 4) * 8 + zh * 2 + c, h)

    other_core = (x * 8 + zh * 2 + (1 - c), h)

    def z_copy(own, full, ss, rs, k):
        return remote(own, full.at[x, zh, c], ss.at[0], rs.at[k // 2], along_z(k))

    def z_own(own, full, sem):
        return pltpu.make_async_copy(own, full.at[x, zh, c], sem)

    def z_start(own, full, ss, rs, sem):
        z_own(own, full, sem).start()
        for k in (1, 3):
            z_copy(own, full, ss, rs, k).start()

    def z_pass(own, full, ss, rs):
        for k in (1, 3):
            came = full.at[x, (zh + 4 - k) % 4, c]
            remote(own, came, ss.at[0], rs.at[k // 2], along_z(k)).wait_recv()
            part = full.at[x, (zh + 4 - k) % 4, c, pl.ds(0 if k == 1 else 8, 8)]
            remote(part, part, ss.at[0], rs.at[2], along_z(k)).start()

    def x_start(own, full, ss, rs, sem):
        z_own(own, full, sem).wait()
        settle(full.at[0, 0, 0], rs.at[2])
        row = full.at[x, :, c]
        for k in (1, 3):
            remote(row, row, ss.at[1], rs.at[3 + k // 2], along_x(k)).start()
        remote(row, row, ss.at[2], rs.at[6], other_core).start()

    def x_pass(full, ss, rs):
        for k in (1, 3):
            xx = (x + 4 - k) % 4
            row = full.at[xx, :, c]
            remote(row, row, ss.at[1], rs.at[3 + k // 2], along_x(k)).wait_recv()
            part = full.at[xx, pl.ds(0 if k == 1 else 2, 2), c]
            remote(part, part, ss.at[1], rs.at[5], along_x(k)).start()
            remote(row, row, ss.at[2], rs.at[6], other_core).start()

    def core_start(full, ss, rs):
        settle(full.at[0, :, 0], rs.at[5])
        row = full.at[(x + 2) % 4, :, c]
        remote(row, row, ss.at[2], rs.at[6], other_core).start()

    def core_arrival(full, rs):
        settle(full.at[:, :, 0], rs.at[6])

    def weights_sent(full, ss):
        settle(full.at[0, pl.ds(0, 3), 0], ss.at[0])
        settle(full.at[pl.ds(0, 3), :, 0], ss.at[1])
        settle(full.at[:, :, 0], ss.at[2])

    @pl.loop(1, NDP)
    def _(o):
        req_copy(o).start()

    z_start(wk_ref, wkf, wk_ss, wk_rs, local_sem.at[0])
    z_start(wv_ref, wvf, wv_ss, wv_rs, local_sem.at[3])
    reqv[pl.ds(me, 1)] = req[pl.ds(me, 1)]
    z_pass(wk_ref, wkf, wk_ss, wk_rs)
    z_pass(wv_ref, wvf, wv_ss, wv_rs)
    settle(reqv.at[pl.ds(0, NDP - 1)], req_r)

    to_smem = pltpu.make_async_copy(reqv, reqs, local_sem.at[1])
    to_smem.start()
    to_smem.wait()
    x_start(wk_ref, wkf, wk_ss, wk_rs, local_sem.at[0])
    fetches[2].wait()
    fetches[3].wait()

    lane8 = lax.broadcasted_iota(jnp.int32, (8, 128), 1)

    def gather(d, own):
        def put(at, value):
            if own:
                rlat0[at] = value[:16]
                rlat1[at] = value[16:]
            else:
                slat[at] = value

        ids = [reqs[d, 0, s] for s in range(CAP)]
        for s in range(CAP):
            put(PART * d + s, pool_ref[ids[s]])
        ropes = [rope_ref[ids[s]] for s in range(CAP)]
        rows = [
            jnp.where(lane8 < 64, ropes[0], ropes[1]),
            jnp.where(lane8 < 64, ropes[2], ropes[3]),
            ropes[4],
            jnp.zeros((8, 128), F32),
        ]
        put(PART * d + CAP, jnp.concatenate(rows, axis=0).astype(BF16))

    def lat_copy(o, chunk):
        p = dp_peer(o)
        rows = pl.ds(chunk * 16, 16)
        return remote(
            slat.at[pl.ds(PART * p, PART), rows],
            rlat[chunk].at[pl.ds(PART * me, PART)],
            lat_s.at[chunk],
            lat_r.at[chunk],
            (p, across(o)),
        )

    @pl.loop(1, 8)
    def _(o):
        gather(dp_peer(o), False)
        lat_copy(o, 0).start()
        lat_copy(o, 1).start()

    x_pass(wkf, wk_ss, wk_rs)
    @pl.loop(8, NDP)
    def _(o):
        gather(dp_peer(o), False)
        lat_copy(o, 0).start()

    core_start(wkf, wk_ss, wk_rs)
    @pl.loop(8, NDP)
    def _(o):
        lat_copy(o, 1).start()

    gather(me, True)

    core_arrival(wkf, wk_rs)

    fetches[4].wait()

    for quad in range(4):
        tiles = []
        for g in range(quad * 4, quad * 4 + 4):
            weight = wkf[:, :, :, g].reshape(LAT, NOPE)
            tiles.append(dot_nt(qn_ref[:, g * NOPE : (g + 1) * NOPE], weight))
        even, odd = by_request(tiles)
        qsend[:, 0, quad * 16 : quad * 16 + 16, :LAT] = even
        qsend[:, 1, quad * 16 : quad * 16 + 16, :LAT] = odd

    def q_copy(k):
        p = head_peer(k)
        rows = pl.ds(h * 64, 64)
        return remote(qsend.at[p // 2, p % 2], qmat.at[rows], q_s, q_r, (me, p))

    for k in OTHERS:
        q_copy(k).start()
    x_start(wv_ref, wvf, wv_ss, wv_rs, local_sem.at[3])
    q_own = pltpu.make_async_copy(
        qsend.at[h // 2, h % 2], qmat.at[pl.ds(h * 64, 64)], local_sem.at[4]
    )
    q_own.start()

    tab_copy.wait()

    def c_copy(r, chunk):
        rows = pl.ds(h * 64, 64)
        features = pl.ds(chunk * 256, 256)
        return remote(
            clat.at[chunk, r], kmat.at[:, rows, features], c_s.at[chunk], c_r.at[chunk], (me, r)
        )

    def cr_copy(r):
        return remote(crope.at[r], kr.at[pl.ds(h * 64, 64)], cr_s, cr_r, (me, r))

    def side(entry, want):
        code = tabs[1, entry]
        value = rropef[code // 2]
        turn = jnp.full((8, 128), code % 2, jnp.int32) != want
        return jnp.where(turn, pltpu.roll(value, 64, 1), value)

    def compact(r, chunk):
        for quarter in range(4):
            rows = pl.ds(quarter * 16, 16)
            for b in range(2):
                entry = r * 16 + b * 8 + quarter * 2
                first = rlat[chunk][tabs[0, entry]].astype(F32)
                second = rlat[chunk][tabs[0, entry + 1]].astype(F32)
                for j in range(2):
                    tile = jnp.concatenate(
                        [first[8 * j : 8 * j + 8], second[8 * j : 8 * j + 8]], axis=0
                    )
                    clat[chunk, r, b, rows, 128 * j : 128 * j + 128] = tile.astype(BF16)

    def compact_rope(r):
        for quarter in range(4):
            rows = pl.ds(quarter * 16, 16)
            ropes = []
            for one in range(2):
                entry = r * 16 + quarter * 2 + one
                ropes.append(jnp.where(lane8 < 64, side(entry, 0), side(entry + 8, 1)))
            crope[r, rows, :] = jnp.concatenate(ropes, axis=0).astype(BF16)

    own_rows = pl.ds(h * 64, 64)

    def c_own(chunk):
        return pltpu.make_async_copy(
            clat.at[chunk, h],
            kmat.at[:, own_rows, pl.ds(chunk * 256, 256)],
            local_sem.at[5 + chunk],
        )

    cr_own = pltpu.make_async_copy(crope.at[h], kr.at[own_rows], local_sem.at[1])

    settle(slat.at[pl.ds(0, PART * (NDP - 1)), pl.ds(0, 16)], lat_r.at[0])

    @pl.loop(0, NH)
    def _(k):
        r = head_peer(k)
        compact(r, 0)

        @pl.when(k != 4)
        def _():
            c_copy(r, 0).start()

    c_own(0).start()
    x_pass(wvf, wv_ss, wv_rs)

    settle(slat.at[pl.ds(0, PART * (NDP - 1)), pl.ds(0, 16)], lat_r.at[1])

    @pl.loop(0, NDP)
    def _(d):
        ropes = [rlat0[PART * d + CAP].astype(F32), rlat1[PART * d + CAP].astype(F32)]
        rropef[pl.ds(4 * d, 4)] = jnp.concatenate(ropes, axis=0).reshape(4, 8, 128)

    @pl.loop(0, NH)
    def _(k):
        r = head_peer(k)
        compact(r, 1)
        compact_rope(r)

        @pl.when(k != 4)
        def _():
            c_copy(r, 1).start()
            cr_copy(r).start()

    c_own(1).start()
    cr_own.start()
    core_start(wvf, wv_ss, wv_rs)

    settle(req.at[pl.ds(0, NDP - 1)], req_s)
    for chunk in range(2):
        settle(slat.at[pl.ds(0, PART * (NDP - 1)), pl.ds(0, 16)], lat_s.at[chunk])

    q_own.wait()
    settle(qmat.at[pl.ds(0, 448)], q_r)
    settle(qmat.at[pl.ds(0, 448)], q_s)
    for chunk in range(2):
        c_own(chunk).wait()
        settle(kmat.at[:, pl.ds(0, 448), pl.ds(0, 256)], c_r.at[chunk])
    cr_own.wait()
    settle(kr.at[pl.ds(0, 448)], cr_r)

    length = len_ref[h]
    newl = jnp.concatenate([newl_ref[h], jnp.zeros((112, LAT), BF16)], axis=0)
    place = length + lax.broadcasted_iota(jnp.int32, (8, 128), 0)
    angle_new = place.astype(F32) * freq_ref[...]
    turned_new = rotated(newr_ref[h], jnp.cos(angle_new), jnp.sin(angle_new))
    newr = jnp.concatenate([turned_new, jnp.zeros((120, 128), F32)], axis=0).astype(BF16)
    column = lax.broadcasted_iota(jnp.int32, (1, 512), 1)
    of_entry = (column // 8) % 8
    tokens = []
    for b in range(2):
        moved = jnp.zeros((1, 512), jnp.int32)
        for e in range(8):
            code = tabs[1, h * 16 + b * 8 + e]
            far = (code // 16 + 4 - zh) % 4
            moved = jnp.where(of_entry == e, far, moved)
        part = jnp.where(moved == 2, (column // 64 + 4) % 8, column // 64)
        tokens.append((of_entry + 8 * b) * 64 + part * 8 + column % 8)
    neg = -jnp.inf

    def o_copy(p):
        return remote(osend.at[pl.ds(p * 64, 64)], oall.at[h], o_s, o_r, (me, p))

    def attend(block):
        rows = pl.ds(pl.multiple_of(block * 128, 128), 128)
        q = qmat[rows, :LAT]
        qrot = qmat[rows, LAT:]
        turned = pltpu.roll(qrot.astype(F32), 64, 1).astype(BF16)
        s0 = (dot_nt(q, kmat[0]) + dot_nt(qrot, kr[...])) * SCALE
        s1 = (dot_nt(q, kmat[1]) + dot_nt(turned, kr[...])) * SCALE
        s2 = (dot_nt(q, newl) + dot_nt(qrot, newr)) * SCALE
        s0 = jnp.where(tokens[0] < length, s0, neg)
        s1 = jnp.where(tokens[1] < length, s1, neg)
        step = lax.broadcasted_iota(jnp.int32, (128, 128), 0) % 4
        s2 = jnp.where(lax.broadcasted_iota(jnp.int32, (128, 128), 1) <= step, s2, neg)
        top = jnp.maximum(
            jnp.maximum(jnp.max(s0, axis=1, keepdims=True), jnp.max(s1, axis=1, keepdims=True)),
            jnp.max(s2, axis=1, keepdims=True),
        )
        e0, e1, e2 = jnp.exp(s0 - top), jnp.exp(s1 - top), jnp.exp(s2 - top)
        total = (
            jnp.sum(e0, axis=1, keepdims=True)
            + jnp.sum(e1, axis=1, keepdims=True)
            + jnp.sum(e2, axis=1, keepdims=True)
        )
        inv = 1.0 / total
        o = dot_nn((e0 * inv).astype(BF16), kmat[0])
        o = o + dot_nn((e1 * inv).astype(BF16), kmat[1])
        o = o + dot_nn((e2 * inv).astype(BF16), newl)
        osend[rows, :] = o.astype(BF16)

    @pl.loop(0, 3)
    def _(i):
        half = (zl + 1 + i // 2) % 2
        block = half * 2 + (y // 2 + (i + 1) // 2) % 2
        attend(block)
        for one in range(2):
            p = 2 * block + one
            o_copy(p).start()

    attend(h // 2)
    partner = 2 * (h // 2) + 1 - h % 2
    o_copy(partner).start()
    oall[pl.ds(h, 1)] = osend[pl.ds(pl.multiple_of(h * 64, 64), 64), :].reshape(1, 64, LAT)

    core_arrival(wvf, wv_rs)
    weights_sent(wkf, wk_ss)
    weights_sent(wvf, wv_ss)
    for chunk in range(2):
        settle(kmat.at[:, pl.ds(0, 448), pl.ds(0, 256)], c_s.at[chunk])
    settle(kr.at[pl.ds(0, 448)], cr_s)
    settle(oall.at[pl.ds(0, 7)], o_r)

    first4 = lax.broadcasted_iota(jnp.int32, (4, 8, LAT), 1) < 4
    for quad in range(4):
        rows = pl.ds(quad * 16, 16)
        o_rows = oall[:, rows, :].astype(F32).reshape(4, 2, 16, LAT)
        for pair in range(2):
            even = o_rows[:, 0, pair * 8 : pair * 8 + 8]
            odd = o_rows[:, 1, pair * 8 : pair * 8 + 8]
            a = jnp.where(first4, even, pltpu.roll(odd, 4, 1))
            b = jnp.where(first4, pltpu.roll(even, 4, 1), odd)
            for one, value in enumerate((a, b)):
                g = quad * 4 + pair * 2 + one
                weight = wvf[:, :, :, g].reshape(LAT, DV)
                result = dot_nn(value.reshape(32, LAT).astype(BF16), weight)
                out_ref[:, g * DV : (g + 1) * DV] = result.astype(BF16)

    settle(oall.at[pl.ds(0, 7)], o_s)


def per_device(
    q_nope,
    q_rope,
    new_latent,
    new_rope,
    pool_latent,
    pool_rope,
    kv_weight,
    src_dev,
    src_block,
    lengths,
):
    blocks = pool_latent.shape[0]
    pool = pool_latent.reshape(blocks, 8, 4, 128).transpose(0, 2, 1, 3).reshape(blocks, 32, 128)
    rope = pool_rope.reshape(blocks, 8, ROPE).astype(F32)
    rope = jnp.concatenate([rope, rope], axis=-1)
    requests, steps = q_nope.shape[0], q_nope.shape[1]
    qr = q_rope.reshape(requests * steps, 16 * ROPE)
    new_rot = jnp.pad(new_rope.astype(F32), ((0, 0), (0, 8 - steps), (0, 128 - ROPE)))
    new_lat = jnp.pad(new_latent, ((0, 0), (0, 16 - steps), (0, 0)))
    qn = q_nope.reshape(requests * steps, 16 * NOPE)

    vm = pl.BlockSpec(memory_space=pltpu.VMEM)
    sm = pl.BlockSpec(memory_space=pltpu.SMEM)
    hbm = pl.BlockSpec(memory_space=pl.ANY)
    dma = pltpu.SemaphoreType.DMA
    out = pl.pallas_call(
        kernel,
        out_shape=jax.ShapeDtypeStruct((requests * steps, 16 * DV), BF16),
        in_specs=[vm, vm, sm, vm, hbm, hbm, hbm, hbm, hbm, vm, vm],
        out_specs=vm,
        scratch_shapes=[
            pltpu.VMEM((blocks, 32, 128), BF16),
            pltpu.VMEM((blocks, 8, 128), F32),
            pltpu.VMEM((16, 16, NOPE + DV), BF16),
            pltpu.VMEM((16, 16, NOPE + DV), F32),
            pltpu.VMEM((16, 16, NOPE), BF16),
            pltpu.VMEM((16, 16, DV), BF16),
            pltpu.VMEM((32, 16 * NOPE), BF16),
            pltpu.VMEM((32, 16 * ROPE), BF16),
            dma((5,)),
            pltpu.VMEM((NDP, 1, 128), jnp.int32),
            pltpu.VMEM((8, 128), jnp.int32),
            pltpu.SMEM((8, 128), jnp.int32),
            pltpu.VMEM((NDP, 1, 128), jnp.int32),
            pltpu.SMEM((NDP, 1, 128), jnp.int32),
            pltpu.VMEM((NDP * PART, 32, 128), BF16),
            pltpu.VMEM((NDP * PART, 16, 128), BF16),
            pltpu.VMEM((NDP * PART, 16, 128), BF16),
            pltpu.VMEM((NDP * 4, 8, 128), F32),
            pltpu.VMEM((2, NH, 2, 64, LAT // 2), BF16),
            pltpu.VMEM((NH, 64, 128), BF16),
            pltpu.VMEM((2, 512, LAT), BF16),
            pltpu.VMEM((512, 128), BF16),
            pltpu.VMEM((4, 4, 2, 16, 16, 128), BF16),
            pltpu.VMEM((4, 4, 2, 16, 16, 128), BF16),
            pltpu.VMEM((4, 2, 64, LAT + 128), BF16),
            pltpu.VMEM((512, LAT + 128), BF16),
            pltpu.VMEM((512, LAT), BF16),
            pltpu.VMEM((NH, 64, LAT), BF16),
            dma((7,)),
            dma, dma, dma((2,)), dma((2,)),
            dma((3,)), dma((7,)), dma((3,)), dma((7,)),
            dma, dma, dma((2,)), dma((2,)), dma, dma, dma, dma,
        ],
        compiler_params=pltpu.CompilerParams(
            collective_id=0, has_side_effects=True, vmem_limit_bytes=48 << 20
        ),
    )(
        src_dev.reshape(1, -1), src_block.reshape(1, -1), lengths, jnp.asarray(FREQS),
        pool, rope, kv_weight, qn, qr, new_lat, new_rot,
    )
    return out.reshape(requests, steps, 16 * DV)


def solution(mesh):
    in_specs = (
        P("dp", None, "head"),
        P("dp", None, "head"),
        P("dp", None, None),
        P("dp", None, None),
        P("dp", "head", None),
        P("dp", "head"),
        P("dp", "head", None),
        P("dp", None),
        P("dp"),
        P("dp"),
    )
    out_specs = P("dp", None, "head")
    return jax.shard_map(
        per_device, mesh=mesh, in_specs=in_specs, out_specs=out_specs, check_vma=False
    )
```

```python
import jax
import jax.numpy as jnp
import numpy as np
from jax import lax
from jax.experimental import pallas as pl
from jax.experimental.pallas import tpu as pltpu
from jax.sharding import PartitionSpec as P

LAT = 512
ROPE = 64
NOPE = 128
DV = 128
CAP = 5
PART = CAP + 1
NDP = 32
NH = 8
MESH = pl.DeviceIdType.MESH
F32 = jnp.float32
BF16 = jnp.bfloat16
SCALE = (NOPE + ROPE) ** (-0.5)
OTHERS = (0, 1, 2, 3, 5, 6, 7)


FREQS = np.tile(10000.0 ** (-(2.0 * np.arange(32)) / 64.0), 4).astype(np.float32).reshape(1, 128)


def rotated(values, cosine, sine):
    lane = lax.broadcasted_iota(jnp.int32, values.shape, 1) % 64
    ahead = pltpu.roll(values, 96, 1)
    behind = pltpu.roll(values, 32, 1)
    return values * cosine + jnp.where(lane < 32, -ahead, behind) * sine


def remote(src, dst, send_sem, recv_sem, device):
    return pltpu.make_async_remote_copy(
        src_ref=src,
        dst_ref=dst,
        send_sem=send_sem,
        recv_sem=recv_sem,
        device_id=device,
        device_id_type=MESH,
    )


def settle(like, sem):
    pltpu.make_async_copy(like, like, sem).wait()


def dot_nt(a, b):
    return lax.dot_general(a, b, (((1,), (1,)), ((), ())), preferred_element_type=F32)


def dot_nn(a, b):
    return lax.dot_general(a, b, (((1,), (0,)), ((), ())), preferred_element_type=F32)


def kernel(
    dev_ref, block_ref, len_ref, freq_ref, pool_hbm, rope_hbm, kv_hbm, qn_hbm, qr_hbm,
    newl_ref, newr_ref, out_ref,
    pool_ref, rope_ref, kv_ref, kvf, wk_ref, wv_ref, qn_ref, qr_ref, fetch_sem,
    req, tab, tabs, reqv, reqs, slat, rlat0, rlat1, rropef, clat, crope, kmat, kr, wkf, wvf,
    qsend, qmat, osend, oall,
    local_sem, req_s, req_r, lat_s, lat_r, wk_ss, wk_rs, wv_ss, wv_rs,
    q_s, q_r, c_s, c_r, cr_s, cr_r, o_s, o_r,
):
    rlat = (rlat0, rlat1)
    me = lax.axis_index("dp")
    h = lax.axis_index("head")
    x, zh, c = me // 8, (me // 2) % 4, me % 2

    def dp_peer(o):
        return ((x + 4 - o // 8) % 4) * 8 + ((zh + 4 - (o // 2) % 4) % 4) * 2 + (c + o % 2) % 2

    zl, y = h // 4, h % 4
    flip = (1 - zl) * 4 + y

    def across(o):
        if isinstance(o, int):
            return flip if (o // 2) % 4 == 2 else h
        return jnp.where((o // 2) % 4 == 2, flip, h)

    def head_peer(k):
        return ((zl + 1 + k // 4) % 2) * 4 + (y + k) % 4

    def head_from(k):
        return ((zl + 1 + k // 4) % 2) * 4 + (y + 4 - k % 4) % 4

    fetches = []
    for source, target in (
        (kv_hbm, kv_ref), (qr_hbm, qr_ref), (pool_hbm, pool_ref), (rope_hbm, rope_ref), (qn_hbm, qn_ref)
    ):
        fetches.append(pltpu.make_async_copy(source, target, fetch_sem.at[len(fetches)]))

    barrier = pltpu.get_barrier_semaphore()

    for o in range(1, NDP):
        pl.semaphore_signal(
            barrier, inc=1, device_id=(dp_peer(o), across(o)), device_id_type=MESH
        )

    for k in OTHERS:
        pl.semaphore_signal(barrier, inc=1, device_id=(me, head_peer(k)), device_id_type=MESH)

    for fetch in fetches:
        fetch.start()

    dev = dev_ref[...]
    blk = block_ref[...]
    row = lax.broadcasted_iota(jnp.int32, (128, 128), 0)
    col = lax.broadcasted_iota(jnp.int32, (128, 128), 1)
    dev_rows = jnp.broadcast_to(dev, (128, 128))
    dev_col = jnp.sum(jnp.where(row == col, dev_rows, 0), axis=1, keepdims=True)
    same = jnp.where((dev_col == dev_rows) & (row < col), 1, 0)
    rank = jnp.sum(same, axis=0, keepdims=True)
    source = lax.broadcasted_iota(jnp.int32, (NDP, 128), 0)
    lanes = lax.broadcasted_iota(jnp.int32, (NDP, 128), 1)
    asked = jnp.zeros((NDP, 128), jnp.int32)
    for slot in range(CAP):
        hit = (source == dev) & (rank == slot)
        found = jnp.sum(jnp.where(hit, blk, 0), axis=1, keepdims=True)
        asked = jnp.where(lanes == slot, found, asked)
    req[...] = asked.reshape(NDP, 1, 128)
    tab[0:1, :] = dev * PART + rank
    tab[1:2, :] = dev * 8 + rank
    tab_copy = pltpu.make_async_copy(tab, tabs, local_sem.at[2])
    tab_copy.start()

    fetches[0].wait()
    kvf[...] = kv_ref[...].astype(F32)
    for g in range(16):
        one_head = kvf[:, g, :]
        wk_ref[g] = one_head[:, :NOPE].astype(BF16)
        wv_ref[g] = one_head[:, NOPE:].astype(BF16)

    fetches[1].wait()
    low = lax.broadcasted_iota(jnp.int32, (32, 128), 1) < 64
    request = lax.broadcasted_iota(jnp.int32, (32, 128), 0)
    position = request % 4
    for r in range(8):
        position = position + jnp.where(request // 4 == r, len_ref[r], 0)
    angle = position.astype(F32) * freq_ref[...]
    cosine, sine = jnp.cos(angle), jnp.sin(angle)

    def by_request(tiles):
        width = tiles[0].shape[-1]
        first = lax.broadcasted_iota(jnp.int32, (4, 8, width), 1) < 4
        even, odd = [], []
        for pair in range(2):
            a = tiles[2 * pair].reshape(4, 8, width)
            b = tiles[2 * pair + 1].reshape(4, 8, width)
            even.append(jnp.where(first, a, pltpu.roll(b, 4, 1)))
            odd.append(jnp.where(first, pltpu.roll(a, 4, 1), b))
        return (
            jnp.concatenate(even, axis=1).astype(BF16),
            jnp.concatenate(odd, axis=1).astype(BF16),
        )

    for quad in range(4):
        tiles = []
        for pair in range(2):
            at = (quad * 2 + pair) * 128
            turned = rotated(qr_ref[:, at : at + 128].astype(F32), cosine, sine)
            tiles.append(jnp.where(low, turned, 0.0))
            tiles.append(jnp.where(low, pltpu.roll(turned, 64, 1), 0.0))
        even, odd = by_request(tiles)
        qsend[:, 0, quad * 16 : quad * 16 + 16, LAT:] = even
        qsend[:, 1, quad * 16 : quad * 16 + 16, LAT:] = odd

    pl.semaphore_wait(barrier, NDP - 1 + NH - 1)

    def req_copy(o):
        p = dp_peer(o)
        return remote(req.at[p], reqv.at[me], req_s, req_r, (p, across(o)))

    def along_z(k):
        return (x * 8 + ((zh + k) % 4) * 2 + c, h)

    def along_x(k):
        return (((x + k) % 4) * 8 + zh * 2 + c, h)

    other_core = (x * 8 + zh * 2 + (1 - c), h)

    def z_copy(own, full, ss, rs, k):
        return remote(own, full.at[x, zh, c], ss.at[0], rs.at[k // 2], along_z(k))

    def z_own(own, full, sem):
        return pltpu.make_async_copy(own, full.at[x, zh, c], sem)

    def z_start(own, full, ss, rs, sem):
        z_own(own, full, sem).start()
        for k in (1, 3):
            z_copy(own, full, ss, rs, k).start()

    def z_pass(own, full, ss, rs):
        for k in (1, 3):
            came = full.at[x, (zh + 4 - k) % 4, c]
            remote(own, came, ss.at[0], rs.at[k // 2], along_z(k)).wait_recv()
            part = full.at[x, (zh + 4 - k) % 4, c, pl.ds(0 if k == 1 else 8, 8)]
            remote(part, part, ss.at[0], rs.at[2], along_z(k)).start()

    def x_start(own, full, ss, rs, sem):
        z_own(own, full, sem).wait()
        settle(full.at[0, 0, 0], rs.at[2])
        row = full.at[x, :, c]
        for k in (1, 3):
            remote(row, row, ss.at[1], rs.at[3 + k // 2], along_x(k)).start()
        remote(row, row, ss.at[2], rs.at[6], other_core).start()

    def x_pass(full, ss, rs):
        for k in (1, 3):
            xx = (x + 4 - k) % 4
            row = full.at[xx, :, c]
            remote(row, row, ss.at[1], rs.at[3 + k // 2], along_x(k)).wait_recv()
            part = full.at[xx, pl.ds(0 if k == 1 else 2, 2), c]
            remote(part, part, ss.at[1], rs.at[5], along_x(k)).start()
            remote(row, row, ss.at[2], rs.at[6], other_core).start()

    def core_start(full, ss, rs):
        settle(full.at[0, :, 0], rs.at[5])
        row = full.at[(x + 2) % 4, :, c]
        remote(row, row, ss.at[2], rs.at[6], other_core).start()

    def core_arrival(full, rs):
        settle(full.at[:, :, 0], rs.at[6])

    def weights_sent(full, ss):
        settle(full.at[0, pl.ds(0, 3), 0], ss.at[0])
        settle(full.at[pl.ds(0, 3), :, 0], ss.at[1])
        settle(full.at[:, :, 0], ss.at[2])

    for o in range(1, NDP):
        req_copy(o).start()

    z_start(wk_ref, wkf, wk_ss, wk_rs, local_sem.at[0])
    z_start(wv_ref, wvf, wv_ss, wv_rs, local_sem.at[3])
    reqv[pl.ds(me, 1)] = req[pl.ds(me, 1)]
    z_pass(wk_ref, wkf, wk_ss, wk_rs)
    z_pass(wv_ref, wvf, wv_ss, wv_rs)
    settle(reqv.at[pl.ds(0, NDP - 1)], req_r)

    to_smem = pltpu.make_async_copy(reqv, reqs, local_sem.at[1])
    to_smem.start()
    to_smem.wait()
    x_start(wk_ref, wkf, wk_ss, wk_rs, local_sem.at[0])
    fetches[2].wait()
    fetches[3].wait()

    lane8 = lax.broadcasted_iota(jnp.int32, (8, 128), 1)

    def gather(d, own):
        def put(at, value):
            if own:
                rlat0[at] = value[:16]
                rlat1[at] = value[16:]
            else:
                slat[at] = value

        ids = [reqs[d, 0, s] for s in range(CAP)]
        for s in range(CAP):
            put(PART * d + s, pool_ref[ids[s]])
        ropes = [rope_ref[ids[s]] for s in range(CAP)]
        rows = [
            jnp.where(lane8 < 64, ropes[0], ropes[1]),
            jnp.where(lane8 < 64, ropes[2], ropes[3]),
            ropes[4],
            jnp.zeros((8, 128), F32),
        ]
        put(PART * d + CAP, jnp.concatenate(rows, axis=0).astype(BF16))

    def lat_copy(o, chunk):
        p = dp_peer(o)
        rows = pl.ds(chunk * 16, 16)
        return remote(
            slat.at[pl.ds(PART * p, PART), rows],
            rlat[chunk].at[pl.ds(PART * me, PART)],
            lat_s.at[chunk],
            lat_r.at[chunk],
            (p, across(o)),
        )

    @pl.loop(1, 8)
    def _(o):
        gather(dp_peer(o), False)
        lat_copy(o, 0).start()
        lat_copy(o, 1).start()

    @pl.loop(8, NDP)
    def _(o):
        gather(dp_peer(o), False)
        lat_copy(o, 0).start()

    x_pass(wkf, wk_ss, wk_rs)
    core_start(wkf, wk_ss, wk_rs)
    @pl.loop(8, NDP)
    def _(o):
        lat_copy(o, 1).start()

    gather(me, True)

    core_arrival(wkf, wk_rs)

    fetches[4].wait()

    for quad in range(4):
        tiles = []
        for g in range(quad * 4, quad * 4 + 4):
            weight = wkf[:, :, :, g].reshape(LAT, NOPE)
            tiles.append(dot_nt(qn_ref[:, g * NOPE : (g + 1) * NOPE], weight))
        even, odd = by_request(tiles)
        qsend[:, 0, quad * 16 : quad * 16 + 16, :LAT] = even
        qsend[:, 1, quad * 16 : quad * 16 + 16, :LAT] = odd

    def q_copy(k):
        p = head_peer(k)
        rows = pl.ds(h * 64, 64)
        return remote(qsend.at[p // 2, p % 2], qmat.at[rows], q_s, q_r, (me, p))

    for k in OTHERS:
        q_copy(k).start()
    x_start(wv_ref, wvf, wv_ss, wv_rs, local_sem.at[3])
    q_own = pltpu.make_async_copy(
        qsend.at[h // 2, h % 2], qmat.at[pl.ds(h * 64, 64)], local_sem.at[4]
    )
    q_own.start()

    tab_copy.wait()

    def c_copy(r, chunk):
        rows = pl.ds(h * 64, 64)
        features = pl.ds(chunk * 256, 256)
        return remote(
            clat.at[chunk, r], kmat.at[:, rows, features], c_s.at[chunk], c_r.at[chunk], (me, r)
        )

    def cr_copy(r):
        return remote(crope.at[r], kr.at[pl.ds(h * 64, 64)], cr_s, cr_r, (me, r))

    def side(entry, want):
        code = tabs[1, entry]
        value = rropef[code // 2]
        turn = jnp.full((8, 128), code % 2, jnp.int32) != want
        return jnp.where(turn, pltpu.roll(value, 64, 1), value)

    def compact(r, chunk):
        for quarter in range(4):
            rows = pl.ds(quarter * 16, 16)
            for b in range(2):
                entry = r * 16 + b * 8 + quarter * 2
                first = rlat[chunk][tabs[0, entry]].astype(F32)
                second = rlat[chunk][tabs[0, entry + 1]].astype(F32)
                for j in range(2):
                    tile = jnp.concatenate(
                        [first[8 * j : 8 * j + 8], second[8 * j : 8 * j + 8]], axis=0
                    )
                    clat[chunk, r, b, rows, 128 * j : 128 * j + 128] = tile.astype(BF16)

    def compact_rope(r):
        for quarter in range(4):
            rows = pl.ds(quarter * 16, 16)
            ropes = []
            for one in range(2):
                entry = r * 16 + quarter * 2 + one
                ropes.append(jnp.where(lane8 < 64, side(entry, 0), side(entry + 8, 1)))
            crope[r, rows, :] = jnp.concatenate(ropes, axis=0).astype(BF16)

    own_rows = pl.ds(h * 64, 64)

    def c_own(chunk):
        return pltpu.make_async_copy(
            clat.at[chunk, h],
            kmat.at[:, own_rows, pl.ds(chunk * 256, 256)],
            local_sem.at[5 + chunk],
        )

    cr_own = pltpu.make_async_copy(crope.at[h], kr.at[own_rows], local_sem.at[1])

    settle(slat.at[pl.ds(0, PART * (NDP - 1)), pl.ds(0, 16)], lat_r.at[0])

    @pl.loop(0, NH)
    def _(k):
        r = head_peer(k)
        compact(r, 0)

        @pl.when(k != 4)
        def _():
            c_copy(r, 0).start()

    c_own(0).start()
    x_pass(wvf, wv_ss, wv_rs)

    settle(slat.at[pl.ds(0, PART * (NDP - 1)), pl.ds(0, 16)], lat_r.at[1])

    @pl.loop(0, NDP)
    def _(d):
        ropes = [rlat0[PART * d + CAP].astype(F32), rlat1[PART * d + CAP].astype(F32)]
        rropef[pl.ds(4 * d, 4)] = jnp.concatenate(ropes, axis=0).reshape(4, 8, 128)

    @pl.loop(0, NH)
    def _(k):
        r = head_peer(k)
        compact(r, 1)
        compact_rope(r)

        @pl.when(k != 4)
        def _():
            c_copy(r, 1).start()
            cr_copy(r).start()

    c_own(1).start()
    cr_own.start()
    core_start(wvf, wv_ss, wv_rs)

    settle(req.at[pl.ds(0, NDP - 1)], req_s)
    for chunk in range(2):
        settle(slat.at[pl.ds(0, PART * (NDP - 1)), pl.ds(0, 16)], lat_s.at[chunk])

    q_own.wait()
    settle(qmat.at[pl.ds(0, 448)], q_r)
    settle(qmat.at[pl.ds(0, 448)], q_s)
    for chunk in range(2):
        c_own(chunk).wait()
        settle(kmat.at[:, pl.ds(0, 448), pl.ds(0, 256)], c_r.at[chunk])
    cr_own.wait()
    settle(kr.at[pl.ds(0, 448)], cr_r)

    length = len_ref[h]
    newl = jnp.concatenate([newl_ref[h], jnp.zeros((112, LAT), BF16)], axis=0)
    place = length + lax.broadcasted_iota(jnp.int32, (8, 128), 0)
    angle_new = place.astype(F32) * freq_ref[...]
    turned_new = rotated(newr_ref[h], jnp.cos(angle_new), jnp.sin(angle_new))
    newr = jnp.concatenate([turned_new, jnp.zeros((120, 128), F32)], axis=0).astype(BF16)
    column = lax.broadcasted_iota(jnp.int32, (1, 512), 1)
    of_entry = (column // 8) % 8
    tokens = []
    for b in range(2):
        moved = jnp.zeros((1, 512), jnp.int32)
        for e in range(8):
            code = tabs[1, h * 16 + b * 8 + e]
            far = (code // 16 + 4 - zh) % 4
            moved = jnp.where(of_entry == e, far, moved)
        part = jnp.where(moved == 2, (column // 64 + 4) % 8, column // 64)
        tokens.append((of_entry + 8 * b) * 64 + part * 8 + column % 8)
    neg = -jnp.inf

    def o_copy(p):
        return remote(osend.at[pl.ds(p * 64, 64)], oall.at[h], o_s, o_r, (me, p))

    def attend(block):
        rows = pl.ds(pl.multiple_of(block * 128, 128), 128)
        q = qmat[rows, :LAT]
        qrot = qmat[rows, LAT:]
        turned = pltpu.roll(qrot.astype(F32), 64, 1).astype(BF16)
        s0 = (dot_nt(q, kmat[0]) + dot_nt(qrot, kr[...])) * SCALE
        s1 = (dot_nt(q, kmat[1]) + dot_nt(turned, kr[...])) * SCALE
        s2 = (dot_nt(q, newl) + dot_nt(qrot, newr)) * SCALE
        s0 = jnp.where(tokens[0] < length, s0, neg)
        s1 = jnp.where(tokens[1] < length, s1, neg)
        step = lax.broadcasted_iota(jnp.int32, (128, 128), 0) % 4
        s2 = jnp.where(lax.broadcasted_iota(jnp.int32, (128, 128), 1) <= step, s2, neg)
        top = jnp.maximum(
            jnp.maximum(jnp.max(s0, axis=1, keepdims=True), jnp.max(s1, axis=1, keepdims=True)),
            jnp.max(s2, axis=1, keepdims=True),
        )
        e0, e1, e2 = jnp.exp(s0 - top), jnp.exp(s1 - top), jnp.exp(s2 - top)
        total = (
            jnp.sum(e0, axis=1, keepdims=True)
            + jnp.sum(e1, axis=1, keepdims=True)
            + jnp.sum(e2, axis=1, keepdims=True)
        )
        inv = 1.0 / total
        o = dot_nn((e0 * inv).astype(BF16), kmat[0])
        o = o + dot_nn((e1 * inv).astype(BF16), kmat[1])
        o = o + dot_nn((e2 * inv).astype(BF16), newl)
        osend[rows, :] = o.astype(BF16)

    @pl.loop(0, 3)
    def _(i):
        half = (zl + 1 + i // 2) % 2
        block = half * 2 + (y // 2 + (i + 1) // 2) % 2
        attend(block)
        for one in range(2):
            p = 2 * block + one
            o_copy(p).start()

    attend(h // 2)
    partner = 2 * (h // 2) + 1 - h % 2
    o_copy(partner).start()
    oall[pl.ds(h, 1)] = osend[pl.ds(pl.multiple_of(h * 64, 64), 64), :].reshape(1, 64, LAT)

    core_arrival(wvf, wv_rs)
    weights_sent(wkf, wk_ss)
    weights_sent(wvf, wv_ss)
    for chunk in range(2):
        settle(kmat.at[:, pl.ds(0, 448), pl.ds(0, 256)], c_s.at[chunk])
    settle(kr.at[pl.ds(0, 448)], cr_s)
    settle(oall.at[pl.ds(0, 7)], o_r)

    first4 = lax.broadcasted_iota(jnp.int32, (4, 8, LAT), 1) < 4
    for quad in range(4):
        rows = pl.ds(quad * 16, 16)
        o_rows = oall[:, rows, :].astype(F32).reshape(4, 2, 16, LAT)
        for pair in range(2):
            even = o_rows[:, 0, pair * 8 : pair * 8 + 8]
            odd = o_rows[:, 1, pair * 8 : pair * 8 + 8]
            a = jnp.where(first4, even, pltpu.roll(odd, 4, 1))
            b = jnp.where(first4, pltpu.roll(even, 4, 1), odd)
            for one, value in enumerate((a, b)):
                g = quad * 4 + pair * 2 + one
                weight = wvf[:, :, :, g].reshape(LAT, DV)
                result = dot_nn(value.reshape(32, LAT).astype(BF16), weight)
                out_ref[:, g * DV : (g + 1) * DV] = result.astype(BF16)

    settle(oall.at[pl.ds(0, 7)], o_s)


def per_device(
    q_nope,
    q_rope,
    new_latent,
    new_rope,
    pool_latent,
    pool_rope,
    kv_weight,
    src_dev,
    src_block,
    lengths,
):
    blocks = pool_latent.shape[0]
    pool = pool_latent.reshape(blocks, 8, 4, 128).transpose(0, 2, 1, 3).reshape(blocks, 32, 128)
    rope = pool_rope.reshape(blocks, 8, ROPE).astype(F32)
    rope = jnp.concatenate([rope, rope], axis=-1)
    requests, steps = q_nope.shape[0], q_nope.shape[1]
    qr = q_rope.reshape(requests * steps, 16 * ROPE)
    new_rot = jnp.pad(new_rope.astype(F32), ((0, 0), (0, 8 - steps), (0, 128 - ROPE)))
    new_lat = jnp.pad(new_latent, ((0, 0), (0, 16 - steps), (0, 0)))
    qn = q_nope.reshape(requests * steps, 16 * NOPE)

    vm = pl.BlockSpec(memory_space=pltpu.VMEM)
    sm = pl.BlockSpec(memory_space=pltpu.SMEM)
    hbm = pl.BlockSpec(memory_space=pl.ANY)
    dma = pltpu.SemaphoreType.DMA
    out = pl.pallas_call(
        kernel,
        out_shape=jax.ShapeDtypeStruct((requests * steps, 16 * DV), BF16),
        in_specs=[vm, vm, sm, vm, hbm, hbm, hbm, hbm, hbm, vm, vm],
        out_specs=vm,
        scratch_shapes=[
            pltpu.VMEM((blocks, 32, 128), BF16),
            pltpu.VMEM((blocks, 8, 128), F32),
            pltpu.VMEM((16, 16, NOPE + DV), BF16),
            pltpu.VMEM((16, 16, NOPE + DV), F32),
            pltpu.VMEM((16, 16, NOPE), BF16),
            pltpu.VMEM((16, 16, DV), BF16),
            pltpu.VMEM((32, 16 * NOPE), BF16),
            pltpu.VMEM((32, 16 * ROPE), BF16),
            dma((5,)),
            pltpu.VMEM((NDP, 1, 128), jnp.int32),
            pltpu.VMEM((8, 128), jnp.int32),
            pltpu.SMEM((8, 128), jnp.int32),
            pltpu.VMEM((NDP, 1, 128), jnp.int32),
            pltpu.SMEM((NDP, 1, 128), jnp.int32),
            pltpu.VMEM((NDP * PART, 32, 128), BF16),
            pltpu.VMEM((NDP * PART, 16, 128), BF16),
            pltpu.VMEM((NDP * PART, 16, 128), BF16),
            pltpu.VMEM((NDP * 4, 8, 128), F32),
            pltpu.VMEM((2, NH, 2, 64, LAT // 2), BF16),
            pltpu.VMEM((NH, 64, 128), BF16),
            pltpu.VMEM((2, 512, LAT), BF16),
            pltpu.VMEM((512, 128), BF16),
            pltpu.VMEM((4, 4, 2, 16, 16, 128), BF16),
            pltpu.VMEM((4, 4, 2, 16, 16, 128), BF16),
            pltpu.VMEM((4, 2, 64, LAT + 128), BF16),
            pltpu.VMEM((512, LAT + 128), BF16),
            pltpu.VMEM((512, LAT), BF16),
            pltpu.VMEM((NH, 64, LAT), BF16),
            dma((7,)),
            dma, dma, dma((2,)), dma((2,)),
            dma((3,)), dma((7,)), dma((3,)), dma((7,)),
            dma, dma, dma((2,)), dma((2,)), dma, dma, dma, dma,
        ],
        compiler_params=pltpu.CompilerParams(
            collective_id=0, has_side_effects=True, vmem_limit_bytes=48 << 20
        ),
    )(
        src_dev.reshape(1, -1), src_block.reshape(1, -1), lengths, jnp.asarray(FREQS),
        pool, rope, kv_weight, qn, qr, new_lat, new_rot,
    )
    return out.reshape(requests, steps, 16 * DV)


def solution(mesh):
    in_specs = (
        P("dp", None, "head"),
        P("dp", None, "head"),
        P("dp", None, None),
        P("dp", None, None),
        P("dp", "head", None),
        P("dp", "head"),
        P("dp", "head", None),
        P("dp", None),
        P("dp"),
        P("dp"),
    )
    out_specs = P("dp", None, "head")
    return jax.shard_map(
        per_device, mesh=mesh, in_specs=in_specs, out_specs=out_specs, check_vma=False
    )
```

```python
import jax
import jax.numpy as jnp
import numpy as np
from jax import lax
from jax.experimental import pallas as pl
from jax.experimental.pallas import tpu as pltpu
from jax.sharding import PartitionSpec as P

LAT = 512
ROPE = 64
NOPE = 128
DV = 128
CAP = 5
PART = CAP + 1
NDP = 32
NH = 8
MESH = pl.DeviceIdType.MESH
F32 = jnp.float32
BF16 = jnp.bfloat16
SCALE = (NOPE + ROPE) ** (-0.5)
OTHERS = (0, 1, 2, 3, 5, 6, 7)


FREQS = np.tile(10000.0 ** (-(2.0 * np.arange(32)) / 64.0), 4).astype(np.float32).reshape(1, 128)


def rotated(values, cosine, sine):
    lane = lax.broadcasted_iota(jnp.int32, values.shape, 1) % 64
    ahead = pltpu.roll(values, 96, 1)
    behind = pltpu.roll(values, 32, 1)
    return values * cosine + jnp.where(lane < 32, -ahead, behind) * sine


def remote(src, dst, send_sem, recv_sem, device):
    return pltpu.make_async_remote_copy(
        src_ref=src,
        dst_ref=dst,
        send_sem=send_sem,
        recv_sem=recv_sem,
        device_id=device,
        device_id_type=MESH,
    )


def settle(like, sem):
    pltpu.make_async_copy(like, like, sem).wait()


def dot_nt(a, b):
    return lax.dot_general(a, b, (((1,), (1,)), ((), ())), preferred_element_type=F32)


def dot_nn(a, b):
    return lax.dot_general(a, b, (((1,), (0,)), ((), ())), preferred_element_type=F32)


def kernel(
    dev_ref, block_ref, len_ref, freq_ref, pool_hbm, rope_hbm, kv_hbm, qn_hbm, qr_hbm,
    newl_ref, newr_ref, out_ref,
    pool_ref, rope_ref, kv_ref, kvf, wk_ref, wv_ref, qn_ref, qr_ref, fetch_sem,
    req, tab, tabs, reqv, reqs, slat, rlat0, rlat1, rropef, clat, crope, kmat, kr, wkf, wvf,
    qsend, qmat, osend, oall,
    local_sem, req_s, req_r, lat_s, lat_r, wk_ss, wk_rs, wv_ss, wv_rs,
    q_s, q_r, c_s, c_r, cr_s, cr_r, o_s, o_r,
):
    rlat = (rlat0, rlat1)
    me = lax.axis_index("dp")
    h = lax.axis_index("head")
    x, zh, c = me // 8, (me // 2) % 4, me % 2

    def dp_peer(o):
        return ((x + 4 - o // 8) % 4) * 8 + ((zh + 4 - (o // 2) % 4) % 4) * 2 + (c + o % 2) % 2

    zl, y = h // 4, h % 4
    flip = (1 - zl) * 4 + y

    def across(o):
        if isinstance(o, int):
            return flip if (o // 2) % 4 == 2 else h
        return jnp.where((o // 2) % 4 == 2, flip, h)

    def head_peer(k):
        return ((zl + 1 + k // 4) % 2) * 4 + (y + k) % 4

    def head_from(k):
        return ((zl + 1 + k // 4) % 2) * 4 + (y + 4 - k % 4) % 4

    fetches = []
    for source, target in (
        (kv_hbm, kv_ref), (qr_hbm, qr_ref), (pool_hbm, pool_ref), (rope_hbm, rope_ref), (qn_hbm, qn_ref)
    ):
        fetches.append(pltpu.make_async_copy(source, target, fetch_sem.at[len(fetches)]))

    barrier = pltpu.get_barrier_semaphore()

    @pl.loop(1, NDP)
    def _(o):
        pl.semaphore_signal(
            barrier, inc=1, device_id=(dp_peer(o), across(o)), device_id_type=MESH
        )

    for k in OTHERS:
        pl.semaphore_signal(barrier, inc=1, device_id=(me, head_peer(k)), device_id_type=MESH)

    for fetch in fetches:
        fetch.start()

    dev = dev_ref[...]
    blk = block_ref[...]
    row = lax.broadcasted_iota(jnp.int32, (128, 128), 0)
    col = lax.broadcasted_iota(jnp.int32, (128, 128), 1)
    dev_rows = jnp.broadcast_to(dev, (128, 128))
    dev_col = jnp.sum(jnp.where(row == col, dev_rows, 0), axis=1, keepdims=True)
    same = jnp.where((dev_col == dev_rows) & (row < col), 1, 0)
    rank = jnp.sum(same, axis=0, keepdims=True)
    source = lax.broadcasted_iota(jnp.int32, (NDP, 128), 0)
    lanes = lax.broadcasted_iota(jnp.int32, (NDP, 128), 1)
    asked = jnp.zeros((NDP, 128), jnp.int32)
    for slot in range(CAP):
        hit = (source == dev) & (rank == slot)
        found = jnp.sum(jnp.where(hit, blk, 0), axis=1, keepdims=True)
        asked = jnp.where(lanes == slot, found, asked)
    req[...] = asked.reshape(NDP, 1, 128)
    tab[0:1, :] = dev * PART + rank
    tab[1:2, :] = dev * 8 + rank
    tab_copy = pltpu.make_async_copy(tab, tabs, local_sem.at[2])
    tab_copy.start()

    fetches[0].wait()
    kvf[...] = kv_ref[...].astype(F32)
    for g in range(16):
        one_head = kvf[:, g, :]
        wk_ref[g] = one_head[:, :NOPE].astype(BF16)
        wv_ref[g] = one_head[:, NOPE:].astype(BF16)

    fetches[1].wait()
    low = lax.broadcasted_iota(jnp.int32, (32, 128), 1) < 64
    request = lax.broadcasted_iota(jnp.int32, (32, 128), 0)
    position = request % 4
    for r in range(8):
        position = position + jnp.where(request // 4 == r, len_ref[r], 0)
    angle = position.astype(F32) * freq_ref[...]
    cosine, sine = jnp.cos(angle), jnp.sin(angle)

    def by_request(tiles):
        width = tiles[0].shape[-1]
        first = lax.broadcasted_iota(jnp.int32, (4, 8, width), 1) < 4
        even, odd = [], []
        for pair in range(2):
            a = tiles[2 * pair].reshape(4, 8, width)
            b = tiles[2 * pair + 1].reshape(4, 8, width)
            even.append(jnp.where(first, a, pltpu.roll(b, 4, 1)))
            odd.append(jnp.where(first, pltpu.roll(a, 4, 1), b))
        return (
            jnp.concatenate(even, axis=1).astype(BF16),
            jnp.concatenate(odd, axis=1).astype(BF16),
        )

    for quad in range(4):
        tiles = []
        for pair in range(2):
            at = (quad * 2 + pair) * 128
            turned = rotated(qr_ref[:, at : at + 128].astype(F32), cosine, sine)
            tiles.append(jnp.where(low, turned, 0.0))
            tiles.append(jnp.where(low, pltpu.roll(turned, 64, 1), 0.0))
        even, odd = by_request(tiles)
        qsend[:, 0, quad * 16 : quad * 16 + 16, LAT:] = even
        qsend[:, 1, quad * 16 : quad * 16 + 16, LAT:] = odd

    pl.semaphore_wait(barrier, NDP - 1 + NH - 1)

    def req_copy(o):
        p = dp_peer(o)
        return remote(req.at[p], reqv.at[me], req_s, req_r, (p, across(o)))

    def along_z(k):
        return (x * 8 + ((zh + k) % 4) * 2 + c, h)

    def along_x(k):
        return (((x + k) % 4) * 8 + zh * 2 + c, h)

    other_core = (x * 8 + zh * 2 + (1 - c), h)

    def z_copy(own, full, ss, rs, k):
        return remote(own, full.at[x, zh, c], ss.at[0], rs.at[k // 2], along_z(k))

    def z_own(own, full, sem):
        return pltpu.make_async_copy(own, full.at[x, zh, c], sem)

    def z_start(own, full, ss, rs, sem):
        z_own(own, full, sem).start()
        for k in (1, 3):
            z_copy(own, full, ss, rs, k).start()

    def z_pass(own, full, ss, rs):
        for k in (1, 3):
            came = full.at[x, (zh + 4 - k) % 4, c]
            remote(own, came, ss.at[0], rs.at[k // 2], along_z(k)).wait_recv()
            part = full.at[x, (zh + 4 - k) % 4, c, pl.ds(0 if k == 1 else 8, 8)]
            remote(part, part, ss.at[0], rs.at[2], along_z(k)).start()

    def x_start(own, full, ss, rs, sem):
        z_own(own, full, sem).wait()
        settle(full.at[0, 0, 0], rs.at[2])
        row = full.at[x, :, c]
        for k in (1, 3):
            remote(row, row, ss.at[1], rs.at[3 + k // 2], along_x(k)).start()
        remote(row, row, ss.at[2], rs.at[6], other_core).start()

    def x_pass(full, ss, rs):
        for k in (1, 3):
            xx = (x + 4 - k) % 4
            row = full.at[xx, :, c]
            remote(row, row, ss.at[1], rs.at[3 + k // 2], along_x(k)).wait_recv()
            part = full.at[xx, pl.ds(0 if k == 1 else 2, 2), c]
            remote(part, part, ss.at[1], rs.at[5], along_x(k)).start()
            remote(row, row, ss.at[2], rs.at[6], other_core).start()

    def core_start(full, ss, rs):
        settle(full.at[0, :, 0], rs.at[5])
        row = full.at[(x + 2) % 4, :, c]
        remote(row, row, ss.at[2], rs.at[6], other_core).start()

    def core_arrival(full, rs):
        settle(full.at[:, :, 0], rs.at[6])

    def weights_sent(full, ss):
        settle(full.at[0, pl.ds(0, 3), 0], ss.at[0])
        settle(full.at[pl.ds(0, 3), :, 0], ss.at[1])
        settle(full.at[:, :, 0], ss.at[2])

    @pl.loop(1, NDP)
    def _(o):
        req_copy(o).start()

    z_start(wk_ref, wkf, wk_ss, wk_rs, local_sem.at[0])
    z_start(wv_ref, wvf, wv_ss, wv_rs, local_sem.at[3])
    reqv[pl.ds(me, 1)] = req[pl.ds(me, 1)]
    z_pass(wk_ref, wkf, wk_ss, wk_rs)
    z_pass(wv_ref, wvf, wv_ss, wv_rs)
    settle(reqv.at[pl.ds(0, NDP - 1)], req_r)

    to_smem = pltpu.make_async_copy(reqv, reqs, local_sem.at[1])
    to_smem.start()
    to_smem.wait()
    x_start(wk_ref, wkf, wk_ss, wk_rs, local_sem.at[0])
    fetches[2].wait()
    fetches[3].wait()

    lane8 = lax.broadcasted_iota(jnp.int32, (8, 128), 1)

    def gather(d, own):
        def put(at, value):
            if own:
                rlat0[at] = value[:16]
                rlat1[at] = value[16:]
            else:
                slat[at] = value

        ids = [reqs[d, 0, s] for s in range(CAP)]
        for s in range(CAP):
            put(PART * d + s, pool_ref[ids[s]])
        ropes = [rope_ref[ids[s]] for s in range(CAP)]
        rows = [
            jnp.where(lane8 < 64, ropes[0], ropes[1]),
            jnp.where(lane8 < 64, ropes[2], ropes[3]),
            ropes[4],
            jnp.zeros((8, 128), F32),
        ]
        put(PART * d + CAP, jnp.concatenate(rows, axis=0).astype(BF16))

    def lat_copy(o, chunk):
        p = dp_peer(o)
        rows = pl.ds(chunk * 16, 16)
        return remote(
            slat.at[pl.ds(PART * p, PART), rows],
            rlat[chunk].at[pl.ds(PART * me, PART)],
            lat_s.at[chunk],
            lat_r.at[chunk],
            (p, across(o)),
        )

    near = (1, 8, 9, 16, 17, 24, 25)
    far = tuple(o for o in range(8, NDP) if (o // 2) % 4)

    def issue(steps, chunks):
        for o in steps:
            if 0 in chunks:
                gather(dp_peer(o), False)
            for chunk in chunks:
                lat_copy(o, chunk).start()

    issue(range(2, 8), (0, 1))
    issue(far, (0,))
    x_pass(wkf, wk_ss, wk_rs)
    issue(near, (0,))
    core_start(wkf, wk_ss, wk_rs)
    issue(far, (1,))
    issue(near, (1,))

    gather(me, True)

    core_arrival(wkf, wk_rs)

    fetches[4].wait()

    for quad in range(4):
        tiles = []
        for g in range(quad * 4, quad * 4 + 4):
            weight = wkf[:, :, :, g].reshape(LAT, NOPE)
            tiles.append(dot_nt(qn_ref[:, g * NOPE : (g + 1) * NOPE], weight))
        even, odd = by_request(tiles)
        qsend[:, 0, quad * 16 : quad * 16 + 16, :LAT] = even
        qsend[:, 1, quad * 16 : quad * 16 + 16, :LAT] = odd

    def q_copy(k):
        p = head_peer(k)
        rows = pl.ds(h * 64, 64)
        return remote(qsend.at[p // 2, p % 2], qmat.at[rows], q_s, q_r, (me, p))

    for k in OTHERS:
        q_copy(k).start()
    x_start(wv_ref, wvf, wv_ss, wv_rs, local_sem.at[3])
    q_own = pltpu.make_async_copy(
        qsend.at[h // 2, h % 2], qmat.at[pl.ds(h * 64, 64)], local_sem.at[4]
    )
    q_own.start()

    tab_copy.wait()

    def c_copy(r, chunk):
        rows = pl.ds(h * 64, 64)
        features = pl.ds(chunk * 256, 256)
        return remote(
            clat.at[chunk, r], kmat.at[:, rows, features], c_s.at[chunk], c_r.at[chunk], (me, r)
        )

    def cr_copy(r):
        return remote(crope.at[r], kr.at[pl.ds(h * 64, 64)], cr_s, cr_r, (me, r))

    def side(entry, want):
        code = tabs[1, entry]
        value = rropef[code // 2]
        turn = jnp.full((8, 128), code % 2, jnp.int32) != want
        return jnp.where(turn, pltpu.roll(value, 64, 1), value)

    def compact(r, chunk):
        for quarter in range(4):
            rows = pl.ds(quarter * 16, 16)
            for b in range(2):
                entry = r * 16 + b * 8 + quarter * 2
                first = rlat[chunk][tabs[0, entry]].astype(F32)
                second = rlat[chunk][tabs[0, entry + 1]].astype(F32)
                for j in range(2):
                    tile = jnp.concatenate(
                        [first[8 * j : 8 * j + 8], second[8 * j : 8 * j + 8]], axis=0
                    )
                    clat[chunk, r, b, rows, 128 * j : 128 * j + 128] = tile.astype(BF16)

    def compact_rope(r):
        for quarter in range(4):
            rows = pl.ds(quarter * 16, 16)
            ropes = []
            for one in range(2):
                entry = r * 16 + quarter * 2 + one
                ropes.append(jnp.where(lane8 < 64, side(entry, 0), side(entry + 8, 1)))
            crope[r, rows, :] = jnp.concatenate(ropes, axis=0).astype(BF16)

    own_rows = pl.ds(h * 64, 64)

    def c_own(chunk):
        return pltpu.make_async_copy(
            clat.at[chunk, h],
            kmat.at[:, own_rows, pl.ds(chunk * 256, 256)],
            local_sem.at[5 + chunk],
        )

    cr_own = pltpu.make_async_copy(crope.at[h], kr.at[own_rows], local_sem.at[1])

    settle(slat.at[pl.ds(0, PART * (NDP - 1)), pl.ds(0, 16)], lat_r.at[0])

    @pl.loop(0, NH)
    def _(k):
        r = head_peer(k)
        compact(r, 0)

        @pl.when(k != 4)
        def _():
            c_copy(r, 0).start()

    c_own(0).start()
    x_pass(wvf, wv_ss, wv_rs)

    settle(slat.at[pl.ds(0, PART * (NDP - 1)), pl.ds(0, 16)], lat_r.at[1])

    @pl.loop(0, NDP)
    def _(d):
        ropes = [rlat0[PART * d + CAP].astype(F32), rlat1[PART * d + CAP].astype(F32)]
        rropef[pl.ds(4 * d, 4)] = jnp.concatenate(ropes, axis=0).reshape(4, 8, 128)

    @pl.loop(0, NH)
    def _(k):
        r = head_peer(k)
        compact(r, 1)
        compact_rope(r)

        @pl.when(k != 4)
        def _():
            c_copy(r, 1).start()
            cr_copy(r).start()

    c_own(1).start()
    cr_own.start()
    core_start(wvf, wv_ss, wv_rs)

    settle(req.at[pl.ds(0, NDP - 1)], req_s)
    for chunk in range(2):
        settle(slat.at[pl.ds(0, PART * (NDP - 1)), pl.ds(0, 16)], lat_s.at[chunk])

    q_own.wait()
    settle(qmat.at[pl.ds(0, 448)], q_r)
    settle(qmat.at[pl.ds(0, 448)], q_s)
    for chunk in range(2):
        c_own(chunk).wait()
        settle(kmat.at[:, pl.ds(0, 448), pl.ds(0, 256)], c_r.at[chunk])
    cr_own.wait()
    settle(kr.at[pl.ds(0, 448)], cr_r)

    length = len_ref[h]
    newl = jnp.concatenate([newl_ref[h], jnp.zeros((112, LAT), BF16)], axis=0)
    place = length + lax.broadcasted_iota(jnp.int32, (8, 128), 0)
    angle_new = place.astype(F32) * freq_ref[...]
    turned_new = rotated(newr_ref[h], jnp.cos(angle_new), jnp.sin(angle_new))
    newr = jnp.concatenate([turned_new, jnp.zeros((120, 128), F32)], axis=0).astype(BF16)
    column = lax.broadcasted_iota(jnp.int32, (1, 512), 1)
    of_entry = (column // 8) % 8
    tokens = []
    for b in range(2):
        moved = jnp.zeros((1, 512), jnp.int32)
        for e in range(8):
            code = tabs[1, h * 16 + b * 8 + e]
            far = (code // 16 + 4 - zh) % 4
            moved = jnp.where(of_entry == e, far, moved)
        part = jnp.where(moved == 2, (column // 64 + 4) % 8, column // 64)
        tokens.append((of_entry + 8 * b) * 64 + part * 8 + column % 8)
    neg = -jnp.inf

    def o_copy(p):
        return remote(osend.at[pl.ds(p * 64, 64)], oall.at[h], o_s, o_r, (me, p))

    def attend(block):
        rows = pl.ds(pl.multiple_of(block * 128, 128), 128)
        q = qmat[rows, :LAT]
        qrot = qmat[rows, LAT:]
        turned = pltpu.roll(qrot.astype(F32), 64, 1).astype(BF16)
        s0 = (dot_nt(q, kmat[0]) + dot_nt(qrot, kr[...])) * SCALE
        s1 = (dot_nt(q, kmat[1]) + dot_nt(turned, kr[...])) * SCALE
        s2 = (dot_nt(q, newl) + dot_nt(qrot, newr)) * SCALE
        s0 = jnp.where(tokens[0] < length, s0, neg)
        s1 = jnp.where(tokens[1] < length, s1, neg)
        step = lax.broadcasted_iota(jnp.int32, (128, 128), 0) % 4
        s2 = jnp.where(lax.broadcasted_iota(jnp.int32, (128, 128), 1) <= step, s2, neg)
        top = jnp.maximum(
            jnp.maximum(jnp.max(s0, axis=1, keepdims=True), jnp.max(s1, axis=1, keepdims=True)),
            jnp.max(s2, axis=1, keepdims=True),
        )
        e0, e1, e2 = jnp.exp(s0 - top), jnp.exp(s1 - top), jnp.exp(s2 - top)
        total = (
            jnp.sum(e0, axis=1, keepdims=True)
            + jnp.sum(e1, axis=1, keepdims=True)
            + jnp.sum(e2, axis=1, keepdims=True)
        )
        inv = 1.0 / total
        o = dot_nn((e0 * inv).astype(BF16), kmat[0])
        o = o + dot_nn((e1 * inv).astype(BF16), kmat[1])
        o = o + dot_nn((e2 * inv).astype(BF16), newl)
        osend[rows, :] = o.astype(BF16)

    @pl.loop(0, 3)
    def _(i):
        half = (zl + 1 + i // 2) % 2
        block = half * 2 + (y // 2 + (i + 1) // 2) % 2
        attend(block)
        for one in range(2):
            p = 2 * block + one
            o_copy(p).start()

    attend(h // 2)
    partner = 2 * (h // 2) + 1 - h % 2
    o_copy(partner).start()
    oall[pl.ds(h, 1)] = osend[pl.ds(pl.multiple_of(h * 64, 64), 64), :].reshape(1, 64, LAT)

    core_arrival(wvf, wv_rs)
    weights_sent(wkf, wk_ss)
    weights_sent(wvf, wv_ss)
    for chunk in range(2):
        settle(kmat.at[:, pl.ds(0, 448), pl.ds(0, 256)], c_s.at[chunk])
    settle(kr.at[pl.ds(0, 448)], cr_s)
    settle(oall.at[pl.ds(0, 7)], o_r)

    first4 = lax.broadcasted_iota(jnp.int32, (4, 8, LAT), 1) < 4
    for quad in range(4):
        rows = pl.ds(quad * 16, 16)
        o_rows = oall[:, rows, :].astype(F32).reshape(4, 2, 16, LAT)
        for pair in range(2):
            even = o_rows[:, 0, pair * 8 : pair * 8 + 8]
            odd = o_rows[:, 1, pair * 8 : pair * 8 + 8]
            a = jnp.where(first4, even, pltpu.roll(odd, 4, 1))
            b = jnp.where(first4, pltpu.roll(even, 4, 1), odd)
            for one, value in enumerate((a, b)):
                g = quad * 4 + pair * 2 + one
                weight = wvf[:, :, :, g].reshape(LAT, DV)
                result = dot_nn(value.reshape(32, LAT).astype(BF16), weight)
                out_ref[:, g * DV : (g + 1) * DV] = result.astype(BF16)

    settle(oall.at[pl.ds(0, 7)], o_s)


def per_device(
    q_nope,
    q_rope,
    new_latent,
    new_rope,
    pool_latent,
    pool_rope,
    kv_weight,
    src_dev,
    src_block,
    lengths,
):
    blocks = pool_latent.shape[0]
    pool = pool_latent.reshape(blocks, 8, 4, 128).transpose(0, 2, 1, 3).reshape(blocks, 32, 128)
    rope = pool_rope.reshape(blocks, 8, ROPE).astype(F32)
    rope = jnp.concatenate([rope, rope], axis=-1)
    requests, steps = q_nope.shape[0], q_nope.shape[1]
    qr = q_rope.reshape(requests * steps, 16 * ROPE)
    new_rot = jnp.pad(new_rope.astype(F32), ((0, 0), (0, 8 - steps), (0, 128 - ROPE)))
    new_lat = jnp.pad(new_latent, ((0, 0), (0, 16 - steps), (0, 0)))
    qn = q_nope.reshape(requests * steps, 16 * NOPE)

    vm = pl.BlockSpec(memory_space=pltpu.VMEM)
    sm = pl.BlockSpec(memory_space=pltpu.SMEM)
    hbm = pl.BlockSpec(memory_space=pl.ANY)
    dma = pltpu.SemaphoreType.DMA
    out = pl.pallas_call(
        kernel,
        out_shape=jax.ShapeDtypeStruct((requests * steps, 16 * DV), BF16),
        in_specs=[vm, vm, sm, vm, hbm, hbm, hbm, hbm, hbm, vm, vm],
        out_specs=vm,
        scratch_shapes=[
            pltpu.VMEM((blocks, 32, 128), BF16),
            pltpu.VMEM((blocks, 8, 128), F32),
            pltpu.VMEM((16, 16, NOPE + DV), BF16),
            pltpu.VMEM((16, 16, NOPE + DV), F32),
            pltpu.VMEM((16, 16, NOPE), BF16),
            pltpu.VMEM((16, 16, DV), BF16),
            pltpu.VMEM((32, 16 * NOPE), BF16),
            pltpu.VMEM((32, 16 * ROPE), BF16),
            dma((5,)),
            pltpu.VMEM((NDP, 1, 128), jnp.int32),
            pltpu.VMEM((8, 128), jnp.int32),
            pltpu.SMEM((8, 128), jnp.int32),
            pltpu.VMEM((NDP, 1, 128), jnp.int32),
            pltpu.SMEM((NDP, 1, 128), jnp.int32),
            pltpu.VMEM((NDP * PART, 32, 128), BF16),
            pltpu.VMEM((NDP * PART, 16, 128), BF16),
            pltpu.VMEM((NDP * PART, 16, 128), BF16),
            pltpu.VMEM((NDP * 4, 8, 128), F32),
            pltpu.VMEM((2, NH, 2, 64, LAT // 2), BF16),
            pltpu.VMEM((NH, 64, 128), BF16),
            pltpu.VMEM((2, 512, LAT), BF16),
            pltpu.VMEM((512, 128), BF16),
            pltpu.VMEM((4, 4, 2, 16, 16, 128), BF16),
            pltpu.VMEM((4, 4, 2, 16, 16, 128), BF16),
            pltpu.VMEM((4, 2, 64, LAT + 128), BF16),
            pltpu.VMEM((512, LAT + 128), BF16),
            pltpu.VMEM((512, LAT), BF16),
            pltpu.VMEM((NH, 64, LAT), BF16),
            dma((7,)),
            dma, dma, dma((2,)), dma((2,)),
            dma((3,)), dma((7,)), dma((3,)), dma((7,)),
            dma, dma, dma((2,)), dma((2,)), dma, dma, dma, dma,
        ],
        compiler_params=pltpu.CompilerParams(
            collective_id=0, has_side_effects=True, vmem_limit_bytes=48 << 20
        ),
    )(
        src_dev.reshape(1, -1), src_block.reshape(1, -1), lengths, jnp.asarray(FREQS),
        pool, rope, kv_weight, qn, qr, new_lat, new_rot,
    )
    return out.reshape(requests, steps, 16 * DV)


def solution(mesh):
    in_specs = (
        P("dp", None, "head"),
        P("dp", None, "head"),
        P("dp", None, None),
        P("dp", None, None),
        P("dp", "head", None),
        P("dp", "head"),
        P("dp", "head", None),
        P("dp", None),
        P("dp"),
        P("dp"),
    )
    out_specs = P("dp", None, "head")
    return jax.shard_map(
        per_device, mesh=mesh, in_specs=in_specs, out_specs=out_specs, check_vma=False
    )
```
